32 devices in a mesh: grp: 4 (over x, core), row: 8 (over z, y).
Axes of the slice: x: 2, y: 2, z: 4, core: 2. Of those that a mesh axis runs over, the one named last changes fastest.
Arguments:
- pair_feats: bfloat16 [16, 6, 128, 128, 128], P('grp', None, 'row'), may hold values from -6 to 6
- block_cols: int32 [16, 6], replicated, may hold values from 0 to 15, as said below
- attn_mask: int32 [16, 6], replicated, may hold values from 0 to 1, as said below
- chain_of_row: int32 [16], replicated, may hold values from 0 to 3
- same_chain: float32 [16], replicated, may hold values from -2 to 2
- node_feats: bfloat16 [2048, 768], P('grp'), may hold values from -6 to 6
- node_cotangent: bfloat16 [2048, 768], P('grp'), may hold values from -6 to 6
- tri_weight: bfloat16 [128, 256], replicated, may hold values from -0.5 to 0.5
- gate_weight: bfloat16 [128, 128], replicated, may hold values from -0.5 to 0.5
- tri_out_weight: bfloat16 [64, 128], replicated, may hold values from -0.75 to 0.75
- bias_weight: bfloat16 [128, 16], replicated, may hold values from -0.5 to 0.5
- query_weight: bfloat16 [768, 768], P(None, 'row'), may hold values from -8 to 8
- key_weight: bfloat16 [768, 768], P(None, 'row'), may hold values from -8 to 8
- value_weight: bfloat16 [768, 768], P(None, 'row'), may hold values from -0.21875 to 0.21875
- out_weight: bfloat16 [768, 768], P('row'), may hold values from -0.21875 to 0.21875
Outputs:
- pair_out: bfloat16 [16, 6, 128, 128, 128], P('grp', None, 'row')
- node_out: bfloat16 [2048, 768], P(('grp', 'row'))
- pair_grad: bfloat16 [16, 6, 128, 128, 128], P('grp', None, 'row')
The draws below stay inside these ranges and needn't reach their ends.
Inputs may be any that keep to these rules, and one draw needn't show every extreme that they name: `block_cols`: block row I belongs to chain group I // 4. Its 6 columns are distinct: itself in slot 0, the other block rows of its own group, and 2 block rows of other groups. The rows of one group name block rows of at most 3 other groups and at most 2 distinct block rows of any one other group; some pair of groups reaches 2. `attn_mask`: slot 0 of every block row is 1.
All inputs are finite; a program needn't handle non-finite values.
Results may differ from the reference program's by a relative error of at most 0.025.
Values may be sent and summed in bfloat16 or wider, within the bound.
No kernel may reach another device: no remote copies, remote signals or barrier semaphores. Data moves between devices by JAX's collectives and lax.ppermute only.
A program may use at most 192 MiB of HBM per device.

```python
import jax
import jax.numpy as jnp
from jax import lax

BLK = 128
CZ = 128
CH = 64
DN = 768
HEADS = 16
HD = 48
BR_GRP = 4
KS = 6
CAPX = 2
GROUPS = 4
PARTNERS = 3
NBR = 16
NRES = 2048


def permutations(subkey, how_many, length):
    subkeys = jax.random.split(subkey, how_many)
    return jax.vmap(lambda single: jax.random.permutation(single, length))(subkeys)


def draw_block_cols(key, part):
    branches = jax.random.split(jax.random.fold_in(key, 101), 4)
    groups = jnp.arange(GROUPS, dtype=jnp.int32)
    inner_rows = jnp.arange(BR_GRP, dtype=jnp.int32)
    local_order = (inner_rows[:, None] + inner_rows[None, :]) % BR_GRP
    own_rows = groups[:, None, None] * BR_GRP + local_order[None, :, :]
    offsets = permutations(branches[0], GROUPS, GROUPS - 1)[:, :PARTNERS].astype(jnp.int32) + 1
    partner = (groups[:, None] + offsets) % GROUPS
    picked_rows = permutations(branches[1], GROUPS * PARTNERS, BR_GRP)[:, :CAPX].astype(jnp.int32)
    union_rows = (partner.reshape(GROUPS * PARTNERS, 1) * BR_GRP + picked_rows).reshape(GROUPS, PARTNERS * CAPX)
    pick_order = permutations(branches[2], GROUPS * BR_GRP, PARTNERS * CAPX).astype(jnp.int32)
    pick_order = pick_order.reshape(GROUPS, BR_GRP, PARTNERS * CAPX)
    pick_order = pick_order.at[:, 0, :].set(jnp.arange(PARTNERS * CAPX, dtype=jnp.int32))
    spread_union = jnp.broadcast_to(union_rows[:, None, :], (GROUPS, BR_GRP, PARTNERS * CAPX))
    interface = jnp.take_along_axis(spread_union, pick_order, axis=2)[:, :, :KS - BR_GRP]
    listed = jnp.concatenate([own_rows, interface], axis=2)
    tail_slots = permutations(branches[3], GROUPS * BR_GRP, KS - 1).astype(jnp.int32).reshape(GROUPS, BR_GRP, KS - 1) + 1
    shuffle = jnp.concatenate([jnp.zeros((GROUPS, BR_GRP, 1), jnp.int32), tail_slots], axis=2)
    return jnp.take_along_axis(listed, shuffle, axis=2).reshape(NBR, KS).astype(jnp.int32)


def draw_attn_mask(key, part):
    levels = jax.random.randint(jax.random.fold_in(key, 202), (NBR, KS), 0, 4)
    allowed = (levels > 0).astype(jnp.int32)
    return allowed.at[:, 0].set(1)


def draw_node_feats(key, part):
    branch = jax.random.fold_in(key, 303)
    values = jax.random.normal(jax.random.fold_in(branch, 1), (NRES, DN), jnp.float32)
    return jnp.clip(values, -6.0, 6.0).astype(jnp.bfloat16)


def query_key(key):
    branch = jax.random.fold_in(key, 404)
    query_part = jax.random.normal(jax.random.fold_in(branch, 1), (DN, DN), jnp.float32) * DN ** (-0.5)
    key_part = jax.random.normal(jax.random.fold_in(branch, 2), (DN, DN), jnp.float32) * DN ** (-0.5)
    return (query_part, key_part)


def draw_query_weight(key, part):
    query_part, key_part = query_key(key)
    return jnp.clip(query_part, -8.0, 8.0).astype(jnp.bfloat16)


def draw_key_weight(key, part):
    return jnp.clip(query_key(key)[1], -8.0, 8.0).astype(jnp.bfloat16)


def touch_ends(entries, stream_key, low, top_value):
    index_at = [jax.random.randint(jax.random.fold_in(stream_key, axis), (), 0, length) for axis, length in enumerate(entries.shape)]
    longest = entries.shape.index(max(entries.shape))
    next_to = index_at[:longest] + [(index_at[longest] + 1) % entries.shape[longest]] + index_at[longest + 1:]
    return entries.at[tuple(index_at)].set(low).at[tuple(next_to)].set(top_value)


def block_levels(stream_key, shape, shards, least, high):
    factor_of, own = 1.0, jax.random.fold_in(stream_key, 6)
    for dim, shards_of in shards:
        heights = jnp.exp(jax.random.uniform(jax.random.fold_in(own, dim), (shards_of,), jnp.float32, least / len(shards), high / len(shards)))
        factor_of = factor_of * jnp.repeat(heights, shape[dim] // shards_of).reshape([-1 if axis == dim else 1 for axis in range(len(shape))])
    return factor_of


def bell_draw(own_key, shape, scale, bound, cuts=(), held_as=jnp.bfloat16):
    array = scale * jax.random.normal(own_key, shape, jnp.float32)
    if cuts:
        array = array * block_levels(own_key, shape, cuts, -0.22, 0.18)
    return jnp.clip(array, -bound, bound).astype(held_as)


def setup_inputs(seed: int = 0) -> dict:
    key_of = jax.random.split(jax.random.key(seed), 16)
    return {
        "pair_feats": bell_draw(key_of[0], (NBR, KS, BLK, BLK, CZ), 1.0, 6.0, ((0, 4), (2, 8))),
        "block_cols": draw_block_cols(jax.random.fold_in(key_of[15], 71), 0),
        "attn_mask": draw_attn_mask(jax.random.fold_in(key_of[15], 71), 0),
        "chain_of_row": touch_ends(jax.random.randint(key_of[3], (NBR,), 0, 4), jax.random.fold_in(key_of[3], 1), 0, 3).astype(jnp.int32),
        "same_chain": jnp.clip(jax.random.uniform(key_of[4], (HEADS,), jnp.float32, -2.0, 2.0), -2.0, 2.0),
        "node_feats": draw_node_feats(jax.random.fold_in(key_of[15], 71), 0),
        "node_cotangent": bell_draw(key_of[6], (NRES, DN), 1.0, 6.0, ((0, 4),)),
        "tri_weight": bell_draw(key_of[7], (CZ, 4 * CH), CZ ** -0.5, 0.5),
        "gate_weight": bell_draw(key_of[8], (CZ, CZ), CZ ** -0.5, 0.5),
        "tri_out_weight": bell_draw(key_of[9], (CH, CZ), CH ** -0.5, 0.75),
        "bias_weight": bell_draw(key_of[10], (CZ, HEADS), CZ ** -0.5, 0.5),
        "query_weight": draw_query_weight(jax.random.fold_in(key_of[15], 71), 0),
        "key_weight": draw_key_weight(jax.random.fold_in(key_of[15], 71), 0),
        "value_weight": bell_draw(key_of[13], (DN, DN), DN ** -0.5, 0.21875, ((1, 8),)),
        "out_weight": bell_draw(key_of[14], (DN, DN), DN ** -0.5, 0.21875, ((0, 8),)),
    }


epsilon = 1e-05

def rounded(values):
    return lax.optimization_barrier(values.astype(jnp.bfloat16))

def norm_parts(values, dimension):
    center = lax.optimization_barrier(jnp.mean(values, axis=dimension, keepdims=True))
    shifted = values - center
    spread = lax.optimization_barrier(jnp.mean(shifted * shifted, axis=dimension, keepdims=True))
    inverse = lax.rsqrt(spread + epsilon)
    return (shifted * inverse, inverse)

def reference(pair_feats, block_cols, attn_mask, chain_of_row, same_chain, node_feats, node_cotangent, tri_weight, gate_weight, tri_out_weight, bias_weight, query_weight, key_weight, value_weight, out_weight):
    tri_float = tri_weight.astype(jnp.float32)
    gate_float = gate_weight.astype(jnp.float32)
    tri_out_float = tri_out_weight.astype(jnp.float32)
    bias_float = bias_weight.astype(jnp.float32)

    def project_row(pair_row):
        normed = rounded(norm_parts(pair_row.astype(jnp.float32), 3)[0]).astype(jnp.float32)
        projected = jnp.einsum('sijc,cx->sxij', normed, tri_float)
        left_proj = rounded(jax.nn.sigmoid(projected[:, CH:2 * CH]) * projected[:, :CH])
        right_proj = rounded(jax.nn.sigmoid(projected[:, 3 * CH:]) * projected[:, 2 * CH:3 * CH])
        bias_rows = rounded(jnp.einsum('sijc,ch->shij', normed, bias_float))
        return (left_proj, right_proj, bias_rows)
    left_all, right_all, bias_all = lax.map(project_row, pair_feats)

    def triangle_row(position):
        left_row = left_all[position].astype(jnp.float32)
        row_cols = block_cols[position]

        def one_slot(column):
            far_row = right_all[column].astype(jnp.float32)
            matches = (row_cols[:, None] == block_cols[column][None, :]).astype(jnp.float32)
            aligned = jnp.einsum('tu,udjk->tdjk', matches, far_row)
            return rounded(jnp.einsum('tdik,tdjk->dij', left_row, aligned))
        return lax.map(one_slot, row_cols)
    tri_all = lax.map(triangle_row, jnp.arange(NBR, dtype=jnp.int32))
    node_norm = rounded(norm_parts(node_feats.astype(jnp.float32), 1)[0])
    queries = rounded(jnp.dot(node_norm, query_weight, preferred_element_type=jnp.float32)).reshape(NBR, BLK, HEADS, HD)
    keys_all = rounded(jnp.dot(node_norm, key_weight, preferred_element_type=jnp.float32)).reshape(NBR, BLK, HEADS, HD)
    values_all = rounded(jnp.dot(node_norm, value_weight, preferred_element_type=jnp.float32)).reshape(NBR, BLK, HEADS, HD)
    cot_heads = rounded(jnp.dot(node_cotangent, out_weight.T, preferred_element_type=jnp.float32)).reshape(NBR, BLK, HEADS, HD)
    score_scale = HD ** (-0.5)

    def attend_row(position):
        row_cols = block_cols[position]
        query_rows = queries[position].astype(jnp.float32)
        near_keys = keys_all[row_cols].astype(jnp.float32)
        near_values = values_all[row_cols].astype(jnp.float32)
        same_flag = (chain_of_row[row_cols] == chain_of_row[position]).astype(jnp.float32)
        scores = jnp.einsum('ihd,sjhd->shij', query_rows, near_keys) * score_scale
        scores = scores + bias_all[position].astype(jnp.float32) + same_chain[None, :, None, None] * same_flag[:, None, None, None]
        scores = jnp.where((attn_mask[position] > 0)[:, None, None, None], scores, -jnp.inf)
        row_top = lax.optimization_barrier(jnp.max(scores, axis=(0, 3), keepdims=True))
        exp_scores = jnp.exp(scores - row_top)
        probabilities = exp_scores / lax.optimization_barrier(jnp.sum(exp_scores, axis=(0, 3), keepdims=True))
        probs_low = rounded(probabilities).astype(jnp.float32)
        mixed_heads = rounded(jnp.einsum('shij,sjhd->ihd', probs_low, near_values)).reshape(BLK, DN)
        grad_probs = jnp.einsum('ihd,sjhd->shij', cot_heads[position].astype(jnp.float32), near_values)
        row_total = lax.optimization_barrier(jnp.sum(probabilities * grad_probs, axis=(0, 3), keepdims=True))
        grad_scores = rounded(probabilities * (grad_probs - row_total))
        return (mixed_heads, grad_scores)
    mixed_rows, grad_blocks = lax.map(attend_row, jnp.arange(NBR, dtype=jnp.int32))
    node_out = (node_feats.astype(jnp.float32) + jnp.dot(mixed_rows.reshape(NRES, DN), out_weight, preferred_element_type=jnp.float32)).astype(jnp.bfloat16)

    def finish_row(position):
        pair_float = pair_feats[position].astype(jnp.float32)
        normed, pair_scale = norm_parts(pair_float, 3)
        normed_short = rounded(normed).astype(jnp.float32)
        gate_values = rounded(jax.nn.sigmoid(jnp.einsum('sijc,cy->sijy', normed_short, gate_float))).astype(jnp.float32)
        tri_norm = rounded(norm_parts(tri_all[position].astype(jnp.float32), 1)[0]).astype(jnp.float32)
        update = jnp.einsum('sxij,xc->sijc', tri_norm, tri_out_float)
        pair_out = (pair_float + gate_values * update).astype(jnp.bfloat16)
        grad_normed = jnp.einsum('shij,ch->sijc', grad_blocks[position].astype(jnp.float32), bias_float)
        centre_grad = grad_normed - lax.optimization_barrier(jnp.mean(grad_normed, axis=3, keepdims=True))
        projection_mean = lax.optimization_barrier(jnp.mean(grad_normed * normed, axis=3, keepdims=True))
        pair_grad = (pair_scale * (centre_grad - normed * projection_mean)).astype(jnp.bfloat16)
        return (pair_out, pair_grad)
    pair_out, pair_grad = lax.map(finish_row, jnp.arange(NBR, dtype=jnp.int32))
    return (pair_out, node_out, pair_grad)
```

```python
import jax
import jax.numpy as jnp
from jax import lax
from jax.experimental import pallas as pl
from jax.experimental.pallas import tpu as pltpu
from jax.sharding import PartitionSpec as P

CAPX = 2
LEAD = 1
EPS = 1e-05
F32 = jnp.float32
BF16 = jnp.bfloat16
VMEM_BYTES = 56 * 1024 * 1024


def norm_parts(values, dimension):
    center = jnp.mean(values, axis=dimension, keepdims=True)
    shifted = values - center
    spread = jnp.mean(shifted * shifted, axis=dimension, keepdims=True)
    inverse = lax.rsqrt(spread + EPS)
    return (shifted * inverse, inverse)


def chunk_starts(chunks, dimension):
    spans, start = [], 0
    for chunk in chunks:
        spans.append((start, start + chunk.shape[dimension]))
        start = spans[-1][1]
    return spans


def params():
    return pltpu.CompilerParams(vmem_limit_bytes=VMEM_BYTES)


def project_rows(pair_feats, weights_t, parts, first, count, heads):
    slots, rows, block, channels = pair_feats.shape[1:]
    hidden = (weights_t.shape[0] - heads) // 4
    part = hidden // parts
    step_rows = 2

    def body(x_ref, w_ref, left_ref, right_ref, bias_ref, left_buf, right_buf):
        weights = w_ref[...]
        for start in range(0, rows, step_rows):
            x = x_ref[start : start + step_rows].astype(F32).reshape(step_rows * block, channels)
            normed = norm_parts(x, 1)[0].astype(BF16)
            projected = lax.dot_general(
                weights, normed, (((1,), (1,)), ((), ())), preferred_element_type=F32
            )
            left_half = projected[:hidden]
            left = left_half * jnp.tanh(projected[hidden : 2 * hidden]) + left_half
            right_half = projected[2 * hidden : 3 * hidden]
            right = right_half * jnp.tanh(projected[3 * hidden : 4 * hidden]) + right_half
            bias = projected[4 * hidden :].astype(BF16)
            for inner in range(step_rows):
                lanes = slice(inner * block, (inner + 1) * block)
                place = start + inner
                left_buf[:, place, :] = left[:, lanes]
                right_buf[:, place, :] = right[:, lanes]
                bias_ref[place * heads : (place + 1) * heads, :] = bias[:, lanes]
        shape = (parts, part, rows, block)
        left_ref[...] = left_buf[...].astype(BF16).reshape(shape)
        right_ref[...] = right_buf[...].astype(BF16).reshape(shape)

    shipped = jax.ShapeDtypeStruct((parts, count, slots, part, rows, block), BF16)
    shipped_spec = pl.BlockSpec(
        (parts, None, None, part, rows, block), lambda i, s: (0, i, s, 0, 0, 0)
    )
    return pl.pallas_call(
        body,
        grid=(count, slots),
        in_specs=[
            pl.BlockSpec((None, None, rows, block, channels), lambda i, s: (first + i, s, 0, 0, 0)),
            pl.BlockSpec(weights_t.shape, lambda i, s: (0, 0)),
        ],
        out_specs=[
            shipped_spec,
            shipped_spec,
            pl.BlockSpec((None, None, rows * heads, block), lambda i, s: (i, s, 0, 0)),
        ],
        out_shape=[
            shipped,
            shipped,
            jax.ShapeDtypeStruct((count, slots, rows * heads, block), BF16),
        ],
        scratch_shapes=[pltpu.VMEM((hidden, rows, block), F32)] * 2,
        compiler_params=params(),
        name=f"project_{first}",
    )(pair_feats, weights_t)


def pick_blocks(rights, send_row, send_slot, offsets):
    parts, _, _, part, rows, block = rights[0].shape
    _, cap_rows, cap_slots = send_slot.shape
    starts = chunk_starts(rights, 1)

    def body(row_ref, slot_ref, *refs):
        ins, out_refs = refs[: len(rights)], refs[len(rights) :]
        for offset in range(offsets):
            for a in range(cap_rows):
                which = row_ref[offset, a]
                for chunk, (begin, end) in enumerate(starts):

                    @pl.when((which >= begin) & (which < end))
                    def _(chunk=chunk, begin=begin, a=a, offset=offset, which=which):
                        for b in range(cap_slots):
                            slot = slot_ref[offset, a, b]
                            for d in range(parts):
                                out_refs[offset][a * cap_slots + b, d] = ins[chunk][
                                    d, which - begin, slot
                                ]

    out = jax.ShapeDtypeStruct((cap_rows * cap_slots, parts, part, rows, block), BF16)
    smem = pl.BlockSpec(memory_space=pltpu.SMEM)
    vmem = pl.BlockSpec(memory_space=pltpu.VMEM)
    return pl.pallas_call(
        body,
        in_specs=[smem, smem] + [vmem] * len(rights),
        out_specs=[vmem] * offsets,
        out_shape=[out] * offsets,
        compiler_params=params(),
        name="pick_blocks",
    )(send_row, send_slot, *rights)


def triangle_rows(left, rights, arrived, source, place, first, *earlier):
    far = len(arrived)
    parts, count, slots, part, rows, block = left.shape
    starts = chunk_starts(rights, 1)
    held = BF16 if rows % 16 == 0 else F32

    def body(source_ref, place_ref, left_ref, *refs):
        right_refs, refs = refs[: len(rights)], refs[len(rights) :]
        far_refs, (out_ref, table) = refs[:far], refs[far + len(earlier) :]
        at_row = first + pl.program_id(1)
        for s in range(slots):
            origin = source_ref[at_row, s]

            def fill(get, s=s):
                for t in range(slots):
                    there = slice(t * block, (t + 1) * block)
                    at = place_ref[at_row, s, t]

                    @pl.when(at >= 0)
                    def _():
                        for d in range(parts):
                            begin = s * block + d * rows
                            table[begin : begin + rows, there] = get(d, at).astype(held)

                    @pl.when(at < 0)
                    def _():
                        table[s * block : (s + 1) * block, there] = jnp.zeros((block, block), held)

            for chunk, (begin, end) in enumerate(starts):

                @pl.when((origin >= begin) & (origin < end))
                def _(chunk=chunk, begin=begin):
                    fill(lambda d, at: right_refs[chunk][d, origin - begin, at])

            for number in range(far):

                @pl.when(origin == starts[-1][1] + number)
                def _(number=number):
                    fill(lambda d, at: far_refs[number][at, d])

        near = jnp.concatenate(
            [
                jnp.concatenate([left_ref[d, t].astype(held) for d in range(parts)], axis=0)
                for t in range(slots)
            ],
            axis=1,
        ).astype(BF16)
        sums = lax.dot_general(
            near,
            table[...].astype(BF16),
            (((1,), (1,)), ((), ())),
            preferred_element_type=F32,
        )
        for d in range(parts):
            for s in range(slots):
                piece = sums[d * rows : (d + 1) * rows, s * block : (s + 1) * block]
                out_ref[d, s] = piece.astype(BF16)

    smem = pl.BlockSpec(memory_space=pltpu.SMEM)
    row_spec = pl.BlockSpec(
        (parts, None, slots, None, rows, block), lambda c, i: (0, i, 0, c, 0, 0)
    )
    far_spec = pl.BlockSpec(
        arrived[0].shape[:2] + (None, rows, block), lambda c, i: (0, 0, c, 0, 0)
    )
    return pl.pallas_call(
        body,
        grid=(part, count),
        in_specs=[smem] * 2
        + [row_spec]
        + [
            pl.BlockSpec(right.shape[:3] + (None, rows, block), lambda c, i: (0, 0, 0, c, 0, 0))
            for right in rights
        ]
        + [far_spec] * far
        + [pl.BlockSpec(memory_space=pl.ANY)] * len(earlier),
        out_specs=row_spec,
        out_shape=jax.ShapeDtypeStruct(left.shape, BF16),
        scratch_shapes=[pltpu.VMEM((slots * block, slots * block), held)],
        compiler_params=params(),
        name=f"triangle_{first}",
    )(source, place, left, *rights, *arrived, *earlier)


def attend(queries, cots, keys, values, bias_rows, places, masks, flags, chain_bias):
    block_rows, rows, width = queries.shape
    heads = chain_bias.shape[0]
    _, slots, _, block = bias_rows[0].shape
    chunks = len(bias_rows)
    chunk_of = [
        (chunk, I - begin)
        for chunk, (begin, end) in enumerate(chunk_starts(bias_rows, 0))
        for I in range(begin, end)
    ]
    head_size = width // heads
    score_scale = head_size ** (-0.5)

    def body(place_ref, mask_ref, flag_ref, q_ref, c_ref, k_ref, v_ref, chain_ref, *refs):
        bias_refs, (mixed_ref, grad_ref) = refs[:chunks], refs[chunks:]
        row_head = lax.broadcasted_iota(jnp.int32, (heads, width), 0)
        lane_head = lax.broadcasted_iota(jnp.int32, (heads, width), 1) // head_size
        own_head = (row_head == lane_head).astype(F32)
        chain = jnp.concatenate([chain_ref[...]] * rows, axis=0)
        for I, (chunk, inner) in enumerate(chunk_of):

            def spread(ref):
                wide = ref[I].astype(F32)
                return jnp.concatenate(
                    [
                        (jnp.broadcast_to(wide[i : i + 1], (heads, width)) * own_head).astype(BF16)
                        for i in range(rows)
                    ],
                    axis=0,
                )

            q_wide, c_wide = spread(q_ref), spread(c_ref)
            scores, grads = [], []
            for s in range(slots):
                near = place_ref[I, s]
                score = lax.dot_general(
                    q_wide, k_ref[near], (((1,), (1,)), ((), ())), preferred_element_type=F32
                )
                score = score * score_scale + bias_refs[chunk][inner, s].astype(F32) + chain * flag_ref[I, s]
                scores.append(jnp.where(mask_ref[I, s] > 0, score, -jnp.inf))
                grads.append(
                    lax.dot_general(
                        c_wide, v_ref[near], (((1,), (1,)), ((), ())), preferred_element_type=F32
                    )
                )
            scores = jnp.concatenate(scores, axis=1)
            grads = jnp.concatenate(grads, axis=1)
            exps = jnp.exp(scores - jnp.max(scores, axis=1, keepdims=True))
            probs = exps / jnp.sum(exps, axis=1, keepdims=True)
            low = probs.astype(BF16)
            mixed = jnp.zeros((rows * heads, width), F32)
            for s in range(slots):
                mixed = mixed + jnp.dot(
                    low[:, s * block : (s + 1) * block],
                    v_ref[place_ref[I, s]],
                    preferred_element_type=F32,
                )
            mixed = mixed.reshape(rows, heads, width) * own_head[None]
            mixed_ref[I] = jnp.sum(mixed, axis=1).astype(BF16)
            total = jnp.sum(probs * grads, axis=1, keepdims=True)
            score_grads = (probs * (grads - total)).astype(BF16)
            for s in range(slots):
                grad_ref[I, s] = score_grads[:, s * block : (s + 1) * block]

    smem = pl.BlockSpec(memory_space=pltpu.SMEM)
    vmem = pl.BlockSpec(memory_space=pltpu.VMEM)
    return pl.pallas_call(
        body,
        in_specs=[smem] * 3 + [vmem] * (5 + chunks),
        out_specs=[vmem, vmem],
        out_shape=[
            jax.ShapeDtypeStruct((block_rows, rows, width), BF16),
            jax.ShapeDtypeStruct((block_rows, slots, rows * heads, block), BF16),
        ],
        compiler_params=params(),
        name="attend",
    )(places, masks, flags, queries, cots, keys, values, chain_bias, *bias_rows)


def gradient_rows(pair_feats, grads, bias_rows, gate_half, back_weight, heads, first, earlier):
    count = bias_rows.shape[0]
    slots, rows, block, channels = pair_feats.shape[1:]

    def body(x_ref, g_ref, b_ref, gate_ref, back_ref, *refs):
        out_ref, grad_ref = refs[-2:]
        gate_weight, back = gate_ref[...], back_ref[...]
        for i in range(rows):
            xhat, scale = norm_parts(x_ref[i].astype(F32), 1)
            gate = jnp.dot(xhat.astype(BF16), gate_weight, preferred_element_type=F32)
            out_ref[i] = (0.5 * jnp.tanh(gate) + 0.5).astype(BF16)
            g = g_ref[i * heads : (i + 1) * heads]
            b = b_ref[i * heads : (i + 1) * heads]
            cross = jnp.sum(g.astype(F32) * b.astype(F32), axis=0, keepdims=True) / channels
            cross = jnp.broadcast_to(cross, (heads, block)).astype(BF16)
            both = lax.dot_general(
                jnp.concatenate([g, cross], axis=0),
                back,
                (((0,), (0,)), ((), ())),
                preferred_element_type=F32,
            )
            centred, projection = both[:, :channels], both[:, channels:]
            grad_ref[i] = (scale * (centred - xhat * projection)).astype(BF16)

    big = pl.BlockSpec((None, None, rows, block, channels), lambda i, s: (first + i, s, 0, 0, 0))
    whole = jax.ShapeDtypeStruct(pair_feats.shape, BF16)
    anywhere = pl.BlockSpec(memory_space=pl.ANY)
    return pl.pallas_call(
        body,
        grid=(count, slots),
        in_specs=[
            big,
            pl.BlockSpec((None, None, rows * heads, block), lambda i, s: (first + i, s, 0, 0)),
            pl.BlockSpec((None, None, rows * heads, block), lambda i, s: (i, s, 0, 0)),
            pl.BlockSpec(gate_half.shape, lambda i, s: (0, 0)),
            pl.BlockSpec(back_weight.shape, lambda i, s: (0, 0)),
        ]
        + [anywhere] * len(earlier),
        out_specs=[big, big],
        out_shape=[whole, whole],
        input_output_aliases={5 + n: n for n in range(len(earlier))},
        compiler_params=params(),
        name=f"gradient_{first}",
    )(pair_feats, grads, bias_rows, gate_half, back_weight, *earlier)


def finish_rows(pair_feats, gates, tri, tri_out_weight, first):
    slots, rows, block, channels = pair_feats.shape[1:]
    parts, count, _, part, _, _ = tri.shape
    hidden = parts * part

    def body(x_ref, gate_ref, tri_ref, w_ref, out_ref, buf):
        sums = tri_ref[...].astype(F32).reshape(hidden, rows, block)
        buf[...] = norm_parts(sums, 0)[0]
        weight = w_ref[...]
        for i in range(rows):
            update = lax.dot_general(
                buf[:, i, :].astype(BF16),
                weight,
                (((0,), (0,)), ((), ())),
                preferred_element_type=F32,
            )
            out_ref[i] = (x_ref[i].astype(F32) + gate_ref[i].astype(F32) * update).astype(BF16)

    big = pl.BlockSpec((None, None, rows, block, channels), lambda i, s: (first + i, s, 0, 0, 0))
    return pl.pallas_call(
        body,
        grid=(count, slots),
        in_specs=[
            big,
            big,
            pl.BlockSpec(
                (parts, None, None, part, rows, block), lambda i, s: (0, i, s, 0, 0, 0)
            ),
            pl.BlockSpec(tri_out_weight.shape, lambda i, s: (0, 0)),
        ],
        out_specs=big,
        out_shape=jax.ShapeDtypeStruct(pair_feats.shape, BF16),
        input_output_aliases={1: 0},
        scratch_shapes=[pltpu.VMEM((hidden, rows, block), F32)],
        compiler_params=params(),
        name=f"finish_{first}",
    )(pair_feats, gates, tri, tri_out_weight)


def after(values, *earlier):
    return lax.optimization_barrier((values,) + earlier)[0]


def doubling_steps(axis):
    size = lax.axis_size(axis)
    return [size >> n for n in range(1, size.bit_length())]


def doubled(stacked, axis, steps):
    size = lax.axis_size(axis)
    for step in steps:
        pairs = [(n, n ^ step) for n in range(size)]
        stacked = jnp.concatenate([stacked, lax.ppermute(stacked, axis, pairs)], axis=0)
    return stacked


def doubled_order(axis):
    away = jnp.arange(lax.axis_size(axis), dtype=jnp.int32) ^ lax.axis_index(axis)
    order = jnp.zeros_like(away)
    for number, step in enumerate(doubling_steps(axis)):
        order = order + jnp.where(away & step, 1 << number, 0)
    return order


def make_plan(block_cols, group_index, group_count, block_rows):
    total_rows, slots = block_cols.shape
    offsets = group_count - 1
    cap_slots = slots - block_rows + CAPX
    first_row = group_index * block_rows
    targets = jnp.arange(total_rows, dtype=jnp.int32)
    owner = targets // block_rows
    groups = jnp.arange(group_count, dtype=jnp.int32)
    hits = (block_cols[:, :, None] == targets).astype(jnp.int32)
    union = jnp.max(hits.reshape(group_count, block_rows * slots, total_rows), axis=1)
    named = union * (owner[None, :] != groups[:, None]).astype(jnp.int32)
    by_owner = named.reshape(group_count, group_count, block_rows)
    row_rank = (jnp.cumsum(by_owner, axis=2) - by_owner).reshape(group_count, total_rows)
    useful = jnp.max(union[:, None, None, :] * hits[None], axis=3)
    slot_rank = jnp.cumsum(useful, axis=2) - useful
    to_group = (group_index + 1 + jnp.arange(offsets, dtype=jnp.int32)) % group_count
    locals_ = jnp.arange(block_rows, dtype=jnp.int32)
    named_here = lax.dynamic_slice_in_dim(named, first_row, block_rows, 1)[to_group]
    rank_here = lax.dynamic_slice_in_dim(row_rank, first_row, block_rows, 1)[to_group]
    caps = jnp.arange(CAPX, dtype=jnp.int32)
    chosen = named_here[:, None, :] * (rank_here[:, None, :] == caps[None, :, None])
    send_row = jnp.sum(chosen * locals_, axis=2).astype(jnp.int32)
    useful_here = lax.dynamic_slice_in_dim(useful, first_row, block_rows, 1)[to_group]
    srank_here = lax.dynamic_slice_in_dim(slot_rank, first_row, block_rows, 1)[to_group]
    cap_ids = jnp.arange(cap_slots, dtype=jnp.int32)
    slot_ids = jnp.arange(slots, dtype=jnp.int32)
    picks = useful_here[:, :, None, :] * (
        srank_here[:, :, None, :] == cap_ids[None, None, :, None]
    )
    slot_of = jnp.sum(picks * slot_ids, axis=3)
    send_slot = jnp.sum(chosen[:, :, :, None] * slot_of[:, None, :, :], axis=2).astype(jnp.int32)
    my_rank = lax.dynamic_index_in_dim(row_rank, group_index, 0, keepdims=False)
    my_slot_rank = lax.dynamic_index_in_dim(slot_rank, group_index, 0, keepdims=False)
    distance = (group_index - owner) % group_count
    is_local = distance == 0
    row_source = jnp.where(is_local, targets - first_row, block_rows + distance - 1)
    node_place = jnp.where(
        is_local, targets - first_row, block_rows + (distance - 1) * CAPX + my_rank
    )
    own_cols = lax.dynamic_slice_in_dim(block_cols, first_row, block_rows, 0)
    near_cols = block_cols[own_cols]
    match = near_cols[:, :, None, :] == own_cols[:, None, :, None]
    found = jnp.max(match.astype(jnp.int32), axis=3)
    slot_place = jnp.where(
        is_local[:, None], slot_ids[None, :], my_rank[:, None] * cap_slots + my_slot_rank
    )
    place = jnp.sum(match.astype(jnp.int32) * slot_place[own_cols][:, :, None, :], axis=3)
    tri_place = jnp.where(found > 0, place, -1).astype(jnp.int32)
    tri_source = row_source[own_cols].astype(jnp.int32)
    return (send_row, send_slot, own_cols, tri_source, tri_place, node_place.astype(jnp.int32))


def per_device(
    pair_feats,
    block_cols,
    attn_mask,
    chain_of_row,
    same_chain,
    node_feats,
    node_cotangent,
    tri_weight,
    gate_weight,
    tri_out_weight,
    bias_weight,
    query_weight,
    key_weight,
    value_weight,
    out_weight,
):
    parts = lax.axis_size("row")
    group_count = lax.axis_size("grp")
    group_index = lax.axis_index("grp")
    row_index = lax.axis_index("row")
    block_rows, slots, rows, block, channels = pair_feats.shape
    hidden = tri_weight.shape[1] // 4
    heads = bias_weight.shape[1]
    width = node_feats.shape[1]
    offsets = group_count - 1
    first_row = group_index * block_rows
    send_row, send_slot, own_cols, tri_source, tri_place, node_place = make_plan(
        block_cols, group_index, group_count, block_rows
    )
    rings = [
        [(g, (g + d) % group_count) for g in range(group_count)] for d in range(1, group_count)
    ]

    weights_t = jnp.concatenate([tri_weight.T * 0.5, bias_weight.T], axis=0).astype(BF16)
    own_weights = jnp.stack([query_weight.T, key_weight.T, value_weight.T, out_weight])
    share = own_weights.shape[0] * own_weights.shape[1] // group_count
    own_share = lax.dynamic_slice_in_dim(
        own_weights.reshape(-1, width), group_index * share, share, 0
    )
    row_steps = doubling_steps("row")
    near_share = doubled(own_share[None], "row", row_steps[:1])

    def swap(values, *earlier):
        return lax.all_to_all(
            after(values, *earlier), "row", split_axis=0, concat_axis=0, tiled=True
        )

    groups = [(0, LEAD), (LEAD, block_rows - LEAD)]
    left_0, right_0, bias_0 = project_rows(pair_feats, weights_t, parts, *groups[0], heads)
    right_lead = swap(right_0, near_share)
    left_1, right_1, bias_1 = project_rows(pair_feats, weights_t, parts, *groups[1], heads)
    lefts, rights, biases = (left_0, left_1), (right_0, right_1), (bias_0, bias_1)
    half_share = doubled(near_share, "row", row_steps[1:-1])
    right_rest = swap(rights[1], right_lead, half_share)
    row_share = doubled(half_share, "row", row_steps[-1:])
    all_stack = jnp.swapaxes(doubled(row_share[None], "grp", doubling_steps("grp")), 0, 1)
    row_order, grp_order = doubled_order("row"), doubled_order("grp")
    rights = [right_lead, right_rest]
    left_rest = swap(
        lefts[1], right_rest, all_stack, send_row, send_slot, node_place, tri_source, tri_place
    )
    outgoing = pick_blocks(rights, send_row, send_slot, offsets)
    arrived = [lax.ppermute(v, "grp", ring) for v, ring in zip(outgoing, rings)]
    all_stack = after(all_stack, *outgoing)

    all_weights = all_stack[row_order[:, None], grp_order[None, :]].reshape(
        (parts,) + own_weights.shape
    )

    def full(number):
        return all_weights[:, number].reshape(width, width)

    node_norm = norm_parts(node_feats.astype(F32), 1)[0].astype(BF16)
    norm_blocks = node_norm.reshape(block_rows, block, width)
    far_nodes = [
        lax.ppermute(norm_blocks[send_row[d]], "grp", rings[d]) for d in range(offsets)
    ]
    near_nodes = jnp.concatenate([norm_blocks] + far_nodes, axis=0).reshape(-1, width)

    def times_t(values, weight):
        return lax.dot_general(
            values, weight, (((1,), (1,)), ((), ())), preferred_element_type=F32
        ).astype(BF16)

    keys = times_t(near_nodes, full(1)).reshape(-1, block, width)
    values = times_t(near_nodes, full(2)).reshape(-1, block, width)

    def own_rows(array):
        return lax.dynamic_slice_in_dim(
            array.reshape(block_rows, block, width), row_index * rows, rows, 1
        ).reshape(block_rows * rows, width)

    queries = times_t(own_rows(node_norm), full(0)).reshape(block_rows, rows, width)
    cots = times_t(own_rows(node_cotangent), full(3)).reshape(block_rows, rows, width)
    own_chain = lax.dynamic_slice_in_dim(chain_of_row, first_row, block_rows, 0)
    masks = lax.dynamic_slice_in_dim(attn_mask, first_row, block_rows, 0)
    flags = (chain_of_row[own_cols] == own_chain[:, None]).astype(F32)
    chain_bias = jnp.broadcast_to(same_chain[:, None], (heads, block))
    mixed, grads = attend(
        queries, cots, keys, values, biases, node_place[own_cols], masks, flags, chain_bias
    )
    bias_float = bias_weight.astype(F32)
    centred = (bias_float - jnp.mean(bias_float, axis=0, keepdims=True)).T
    zeros = jnp.zeros((heads, channels), F32)
    back_weight = jnp.concatenate(
        [
            jnp.concatenate([centred, zeros], axis=1),
            jnp.concatenate([zeros, zeros + 1.0 / heads], axis=1),
        ],
        axis=0,
    ).astype(BF16)
    gate_half = (gate_weight * 0.5).astype(BF16)
    whole = ()
    for (first, _), bias in zip(groups, biases):
        whole = gradient_rows(
            pair_feats, grads, bias, gate_half, back_weight, heads, first, whole
        )
    pair_out, pair_grad = whole

    left_lead = swap(lefts[0], left_rest, pair_grad, *arrived)
    sums = triangle_rows(left_rest, rights, arrived, tri_source, tri_place, LEAD)
    tri_rest = swap(sums, left_lead)
    near_mixed = after(mixed[None], sums)
    for step in [1 << n for n in range(block_rows.bit_length() - 1)]:
        other = lax.ppermute(near_mixed, "row", [(r, r ^ step) for r in range(parts)])
        swapped = (row_index & step) > 0
        near_mixed = jnp.concatenate(
            [jnp.where(swapped, other, near_mixed), jnp.where(swapped, near_mixed, other)], axis=0
        )
    sharers = parts // block_rows
    sent_mixed = lax.dynamic_index_in_dim(near_mixed, row_index % block_rows, 1, keepdims=False)
    senders = [((r % sharers) * block_rows + r // sharers, r) for r in range(parts)]
    node_rows = block_rows * block // parts
    mixed_own = lax.ppermute(sent_mixed, "row", senders).reshape(node_rows, width)
    sums = triangle_rows(left_lead, rights, arrived, tri_source, tri_place, 0, mixed_own)
    tri_lead = swap(sums, tri_rest)
    own_nodes = lax.dynamic_slice_in_dim(node_feats, row_index * node_rows, node_rows, 0)
    node_out = (
        own_nodes.astype(F32) + jnp.dot(mixed_own, full(3), preferred_element_type=F32)
    ).astype(BF16)
    tri_lead = after(tri_lead, node_out)
    pair_out = finish_rows(pair_feats, pair_out, tri_rest, tri_out_weight, LEAD)
    pair_out = finish_rows(pair_feats, pair_out, tri_lead, tri_out_weight, 0)
    return (pair_out, node_out, pair_grad)


def solution(mesh):
    pair_spec = P("grp", None, "row", None, None)
    in_specs = (
        (pair_spec,)
        + (P(),) * 4
        + (P("grp", None),) * 2
        + (P(),) * 4
        + (P(None, "row"),) * 3
        + (P("row", None),)
    )
    out_specs = (pair_spec, P(("grp", "row"), None), pair_spec)
    return jax.shard_map(
        per_device, mesh=mesh, in_specs=in_specs, out_specs=out_specs, check_vma=False
    )
```

```python
import jax
import jax.numpy as jnp
from jax import lax
from jax.experimental import pallas as pl
from jax.experimental.pallas import tpu as pltpu
from jax.sharding import PartitionSpec as P

CAPX = 2
LEAD = 1
EPS = 1e-05
F32 = jnp.float32
BF16 = jnp.bfloat16
VMEM_BYTES = 56 * 1024 * 1024


def norm_parts(values, dimension):
    center = jnp.mean(values, axis=dimension, keepdims=True)
    shifted = values - center
    spread = jnp.mean(shifted * shifted, axis=dimension, keepdims=True)
    inverse = lax.rsqrt(spread + EPS)
    return (shifted * inverse, inverse)


def chunk_starts(chunks, dimension):
    spans, start = [], 0
    for chunk in chunks:
        spans.append((start, start + chunk.shape[dimension]))
        start = spans[-1][1]
    return spans


def params():
    return pltpu.CompilerParams(vmem_limit_bytes=VMEM_BYTES)


def project_rows(pair_feats, weights_t, parts, first, count, heads):
    slots, rows, block, channels = pair_feats.shape[1:]
    hidden = (weights_t.shape[0] - heads) // 4
    span = parts // 2
    near, part = hidden // 2, hidden // 2 // parts
    near_part = near // span
    step_rows = 2

    def body(
        x_ref, w_ref, left_near, left_ref, right_near, right_ref, bias_ref, left_buf, right_buf
    ):
        weights = w_ref[...]
        for start in range(0, rows, step_rows):
            x = x_ref[start : start + step_rows].astype(F32).reshape(step_rows * block, channels)
            normed = norm_parts(x, 1)[0].astype(BF16)
            projected = lax.dot_general(
                weights, normed, (((1,), (1,)), ((), ())), preferred_element_type=F32
            )
            left_half = projected[:hidden]
            left = left_half * jnp.tanh(projected[hidden : 2 * hidden]) + left_half
            right_half = projected[2 * hidden : 3 * hidden]
            right = right_half * jnp.tanh(projected[3 * hidden : 4 * hidden]) + right_half
            bias = projected[4 * hidden :].astype(BF16)
            for inner in range(step_rows):
                lanes = slice(inner * block, (inner + 1) * block)
                place = start + inner
                left_buf[:, place, :] = left[:, lanes]
                right_buf[:, place, :] = right[:, lanes]
                bias_ref[place * heads : (place + 1) * heads, :] = bias[:, lanes]
        shape, near_shape = (parts, part, rows, block), (span, near_part, rows, block)
        left_near[...] = left_buf[:near].astype(BF16).reshape(near_shape)
        left_ref[...] = left_buf[near:].astype(BF16).reshape(shape)
        right_half = right_buf[:near].astype(BF16).reshape(near_shape)
        right_near[:span] = right_half
        right_near[span:] = right_half
        right_ref[...] = right_buf[near:].astype(BF16).reshape(shape)

    shapes = [
        (devices, count, slots, channels_here, rows, block)
        for devices, channels_here in (
            (span, near_part),
            (parts, part),
            (parts, near_part),
            (parts, part),
        )
    ]
    return pl.pallas_call(
        body,
        grid=(count, slots),
        in_specs=[
            pl.BlockSpec((None, None, rows, block, channels), lambda i, s: (first + i, s, 0, 0, 0)),
            pl.BlockSpec(weights_t.shape, lambda i, s: (0, 0)),
        ],
        out_specs=[
            pl.BlockSpec(
                (shape[0], None, None) + shape[3:], lambda i, s: (0, i, s, 0, 0, 0)
            )
            for shape in shapes
        ]
        + [pl.BlockSpec((None, None, rows * heads, block), lambda i, s: (i, s, 0, 0))],
        out_shape=[jax.ShapeDtypeStruct(shape, BF16) for shape in shapes]
        + [jax.ShapeDtypeStruct((count, slots, rows * heads, block), BF16)],
        scratch_shapes=[pltpu.VMEM((hidden, rows, block), F32)] * 2,
        compiler_params=params(),
        name=f"project_{first}",
    )(pair_feats, weights_t)


def pick_blocks(rights, send_row, send_slot, offsets):
    parts, _, _, part, rows, block = rights[0].shape
    _, cap_rows, cap_slots = send_slot.shape
    starts = chunk_starts(rights, 1)

    def body(row_ref, slot_ref, *refs):
        ins, out_refs = refs[: len(rights)], refs[len(rights) :]
        for offset in range(offsets):
            for a in range(cap_rows):
                which = row_ref[offset, a]
                for chunk, (begin, end) in enumerate(starts):

                    @pl.when((which >= begin) & (which < end))
                    def _(chunk=chunk, begin=begin, a=a, offset=offset, which=which):
                        for b in range(cap_slots):
                            slot = slot_ref[offset, a, b]
                            for d in range(parts):
                                out_refs[offset][a * cap_slots + b, d] = ins[chunk][
                                    d, which - begin, slot
                                ]

    out = jax.ShapeDtypeStruct((cap_rows * cap_slots, parts, part, rows, block), BF16)
    smem = pl.BlockSpec(memory_space=pltpu.SMEM)
    vmem = pl.BlockSpec(memory_space=pltpu.VMEM)
    return pl.pallas_call(
        body,
        in_specs=[smem, smem] + [vmem] * len(rights),
        out_specs=[vmem] * offsets,
        out_shape=[out] * offsets,
        compiler_params=params(),
        name="pick_blocks",
    )(send_row, send_slot, *rights)


def triangle_rows(lefts, rights, arrived, source, place, first, *earlier):
    far, mine = len(arrived), len(lefts)
    parts = rights[0].shape[0]
    _, count, slots, part, rows, block = lefts[0].shape
    pieces = [(number, n) for number, left in enumerate(lefts) for n in range(left.shape[0])]
    starts = chunk_starts(rights, 1)
    held = BF16 if rows % 16 == 0 else F32

    def body(source_ref, place_ref, *refs):
        left_refs, refs = refs[:mine], refs[mine:]
        right_refs, refs = refs[: len(rights)], refs[len(rights) :]
        far_refs, refs = refs[:far], refs[far + len(earlier) :]
        out_refs, table = refs[:mine], refs[mine]
        at_row = first + pl.program_id(1)
        for s in range(slots):
            origin = source_ref[at_row, s]

            def fill(get, s=s):
                for t in range(slots):
                    there = slice(t * block, (t + 1) * block)
                    at = place_ref[at_row, s, t]

                    @pl.when(at >= 0)
                    def _():
                        for d in range(parts):
                            begin = s * block + d * rows
                            table[begin : begin + rows, there] = get(d, at).astype(held)

                    @pl.when(at < 0)
                    def _():
                        table[s * block : (s + 1) * block, there] = jnp.zeros((block, block), held)

            for chunk, (begin, end) in enumerate(starts):

                @pl.when((origin >= begin) & (origin < end))
                def _(chunk=chunk, begin=begin):
                    fill(lambda d, at: right_refs[chunk][d, origin - begin, at])

            for number in range(far):

                @pl.when(origin == starts[-1][1] + number)
                def _(number=number):
                    fill(lambda d, at: far_refs[number][at, d])

        near = jnp.concatenate(
            [
                jnp.concatenate([left_refs[m][n, t].astype(held) for m, n in pieces], axis=0)
                for t in range(slots)
            ],
            axis=1,
        ).astype(BF16)
        sums = lax.dot_general(
            near,
            table[...].astype(BF16),
            (((1,), (1,)), ((), ())),
            preferred_element_type=F32,
        )
        for d, (m, n) in enumerate(pieces):
            for s in range(slots):
                piece = sums[d * rows : (d + 1) * rows, s * block : (s + 1) * block]
                out_refs[m][n, s] = piece.astype(BF16)

    smem = pl.BlockSpec(memory_space=pltpu.SMEM)
    row_specs = [
        pl.BlockSpec(
            (left.shape[0], None, slots, None, rows, block), lambda c, i: (0, i, 0, c, 0, 0)
        )
        for left in lefts
    ]
    far_spec = pl.BlockSpec(
        arrived[0].shape[:2] + (None, rows, block), lambda c, i: (0, 0, c, 0, 0)
    )
    return pl.pallas_call(
        body,
        grid=(part, count),
        in_specs=[smem] * 2
        + row_specs
        + [
            pl.BlockSpec(right.shape[:3] + (None, rows, block), lambda c, i: (0, 0, 0, c, 0, 0))
            for right in rights
        ]
        + [far_spec] * far
        + [pl.BlockSpec(memory_space=pl.ANY)] * len(earlier),
        out_specs=row_specs,
        out_shape=[jax.ShapeDtypeStruct(left.shape, BF16) for left in lefts],
        scratch_shapes=[pltpu.VMEM((slots * block, slots * block), held)],
        compiler_params=params(),
        name=f"triangle_{first}",
    )(source, place, *lefts, *rights, *arrived, *earlier)


def attend(queries, cots, keys, values, bias_rows, places, masks, flags, chain_bias, *earlier):
    block_rows, rows, width = queries.shape
    heads = chain_bias.shape[0]
    _, slots, _, block = bias_rows[0].shape
    chunks = len(bias_rows)
    chunk_of = [
        (chunk, I - begin)
        for chunk, (begin, end) in enumerate(chunk_starts(bias_rows, 0))
        for I in range(begin, end)
    ]
    head_size = width // heads
    score_scale = head_size ** (-0.5)

    def body(place_ref, mask_ref, flag_ref, q_ref, c_ref, k_ref, v_ref, chain_ref, *refs):
        bias_refs, (mixed_ref, grad_ref) = refs[:chunks], refs[-2:]
        row_head = lax.broadcasted_iota(jnp.int32, (heads, width), 0)
        lane_head = lax.broadcasted_iota(jnp.int32, (heads, width), 1) // head_size
        own_head = (row_head == lane_head).astype(F32)
        chain = jnp.concatenate([chain_ref[...]] * rows, axis=0)
        for I, (chunk, inner) in enumerate(chunk_of):

            def spread(ref):
                wide = ref[I].astype(F32)
                return jnp.concatenate(
                    [
                        (jnp.broadcast_to(wide[i : i + 1], (heads, width)) * own_head).astype(BF16)
                        for i in range(rows)
                    ],
                    axis=0,
                )

            q_wide, c_wide = spread(q_ref), spread(c_ref)
            scores, grads = [], []
            for s in range(slots):
                near = place_ref[I, s]
                score = lax.dot_general(
                    q_wide, k_ref[near], (((1,), (1,)), ((), ())), preferred_element_type=F32
                )
                score = score * score_scale + bias_refs[chunk][inner, s].astype(F32) + chain * flag_ref[I, s]
                scores.append(jnp.where(mask_ref[I, s] > 0, score, -jnp.inf))
                grads.append(
                    lax.dot_general(
                        c_wide, v_ref[near], (((1,), (1,)), ((), ())), preferred_element_type=F32
                    )
                )
            scores = jnp.concatenate(scores, axis=1)
            grads = jnp.concatenate(grads, axis=1)
            exps = jnp.exp(scores - jnp.max(scores, axis=1, keepdims=True))
            probs = exps / jnp.sum(exps, axis=1, keepdims=True)
            low = probs.astype(BF16)
            mixed = jnp.zeros((rows * heads, width), F32)
            for s in range(slots):
                mixed = mixed + jnp.dot(
                    low[:, s * block : (s + 1) * block],
                    v_ref[place_ref[I, s]],
                    preferred_element_type=F32,
                )
            mixed = mixed.reshape(rows, heads, width) * own_head[None]
            mixed_ref[I] = jnp.sum(mixed, axis=1).astype(BF16)
            total = jnp.sum(probs * grads, axis=1, keepdims=True)
            score_grads = (probs * (grads - total)).astype(BF16)
            for s in range(slots):
                grad_ref[I, s] = score_grads[:, s * block : (s + 1) * block]

    smem = pl.BlockSpec(memory_space=pltpu.SMEM)
    vmem = pl.BlockSpec(memory_space=pltpu.VMEM)
    return pl.pallas_call(
        body,
        in_specs=[smem] * 3
        + [vmem] * (5 + chunks)
        + [pl.BlockSpec(memory_space=pl.ANY)] * len(earlier),
        out_specs=[vmem, vmem],
        out_shape=[
            jax.ShapeDtypeStruct((block_rows, rows, width), BF16),
            jax.ShapeDtypeStruct((block_rows, slots, rows * heads, block), BF16),
        ],
        compiler_params=params(),
        name="attend",
    )(places, masks, flags, queries, cots, keys, values, chain_bias, *bias_rows, *earlier)


def gradient_rows(pair_feats, grads, bias_rows, gate_half, back_weight, heads, first, earlier):
    count = bias_rows.shape[0]
    slots, rows, block, channels = pair_feats.shape[1:]

    def body(x_ref, g_ref, b_ref, gate_ref, back_ref, *refs):
        out_ref, grad_ref = refs[-2:]
        gate_weight, back = gate_ref[...], back_ref[...]
        for i in range(rows):
            xhat, scale = norm_parts(x_ref[i].astype(F32), 1)
            gate = jnp.dot(xhat.astype(BF16), gate_weight, preferred_element_type=F32)
            out_ref[i] = (0.5 * jnp.tanh(gate) + 0.5).astype(BF16)
            g = g_ref[i * heads : (i + 1) * heads]
            b = b_ref[i * heads : (i + 1) * heads]
            cross = jnp.sum(g.astype(F32) * b.astype(F32), axis=0, keepdims=True) / channels
            cross = jnp.broadcast_to(cross, (heads, block)).astype(BF16)
            both = lax.dot_general(
                jnp.concatenate([g, cross], axis=0),
                back,
                (((0,), (0,)), ((), ())),
                preferred_element_type=F32,
            )
            centred, projection = both[:, :channels], both[:, channels:]
            grad_ref[i] = (scale * (centred - xhat * projection)).astype(BF16)

    big = pl.BlockSpec((None, None, rows, block, channels), lambda i, s: (first + i, s, 0, 0, 0))
    whole = jax.ShapeDtypeStruct(pair_feats.shape, BF16)
    anywhere = pl.BlockSpec(memory_space=pl.ANY)
    return pl.pallas_call(
        body,
        grid=(count, slots),
        in_specs=[
            big,
            pl.BlockSpec((None, None, rows * heads, block), lambda i, s: (first + i, s, 0, 0)),
            pl.BlockSpec((None, None, rows * heads, block), lambda i, s: (i, s, 0, 0)),
            pl.BlockSpec(gate_half.shape, lambda i, s: (0, 0)),
            pl.BlockSpec(back_weight.shape, lambda i, s: (0, 0)),
        ]
        + [anywhere] * len(earlier),
        out_specs=[big, big],
        out_shape=[whole, whole],
        input_output_aliases={5 + n: n for n in range(len(earlier))},
        compiler_params=params(),
        name=f"gradient_{first}",
    )(pair_feats, grads, bias_rows, gate_half, back_weight, *earlier)


def finish_rows(pair_feats, gates, near_tris, tri, tri_out_weight, place, first):
    slots, rows, block, channels = pair_feats.shape[1:]
    parts, count, _, part, _, _ = tri.shape
    span, near_part = len(near_tris), near_tris[0].shape[3]
    near = span * near_part
    hidden = near + parts * part

    def body(place_ref, x_ref, gate_ref, *refs):
        near_refs, (tri_ref, w_ref, out_ref, buf) = refs[:span], refs[span:]
        for d in range(span):
            here = pl.ds((place_ref[0] ^ d) * near_part, near_part)
            buf[here] = near_refs[d][...].astype(F32)
        buf[near:] = tri_ref[...].astype(F32).reshape(parts * part, rows, block)
        buf[...] = norm_parts(buf[...], 0)[0]
        weight = w_ref[...]
        for i in range(rows):
            update = lax.dot_general(
                buf[:, i, :].astype(BF16),
                weight,
                (((0,), (0,)), ((), ())),
                preferred_element_type=F32,
            )
            out_ref[i] = (x_ref[i].astype(F32) + gate_ref[i].astype(F32) * update).astype(BF16)

    big = pl.BlockSpec((None, None, rows, block, channels), lambda i, s: (first + i, s, 0, 0, 0))
    return pl.pallas_call(
        body,
        grid=(count, slots),
        in_specs=[pl.BlockSpec(memory_space=pltpu.SMEM), big, big]
        + [
            pl.BlockSpec(
                (None, None, None, near_part, rows, block), lambda i, s: (0, i, s, 0, 0, 0)
            )
        ]
        * span
        + [
            pl.BlockSpec(
                (parts, None, None, part, rows, block), lambda i, s: (0, i, s, 0, 0, 0)
            ),
            pl.BlockSpec(tri_out_weight.shape, lambda i, s: (0, 0)),
        ],
        out_specs=big,
        out_shape=jax.ShapeDtypeStruct(pair_feats.shape, BF16),
        input_output_aliases={2: 0},
        scratch_shapes=[pltpu.VMEM((hidden, rows, block), F32)],
        compiler_params=params(),
        name=f"finish_{first}",
    )(place, pair_feats, gates, *near_tris, tri, tri_out_weight)


def after(values, *earlier):
    return lax.optimization_barrier((values,) + earlier)[0]


def doubling_steps(axis):
    size = lax.axis_size(axis)
    return [size >> n for n in range(1, size.bit_length())]


def doubled(stacked, axis, steps):
    size = lax.axis_size(axis)
    for step in steps:
        pairs = [(n, n ^ step) for n in range(size)]
        stacked = jnp.concatenate([stacked, lax.ppermute(stacked, axis, pairs)], axis=0)
    return stacked


def doubled_order(axis):
    away = jnp.arange(lax.axis_size(axis), dtype=jnp.int32) ^ lax.axis_index(axis)
    order = jnp.zeros_like(away)
    for number, step in enumerate(doubling_steps(axis)):
        order = order + jnp.where(away & step, 1 << number, 0)
    return order


def make_plan(block_cols, group_index, group_count, block_rows):
    total_rows, slots = block_cols.shape
    offsets = group_count - 1
    cap_slots = slots - block_rows + CAPX
    first_row = group_index * block_rows
    targets = jnp.arange(total_rows, dtype=jnp.int32)
    owner = targets // block_rows
    groups = jnp.arange(group_count, dtype=jnp.int32)
    hits = (block_cols[:, :, None] == targets).astype(jnp.int32)
    union = jnp.max(hits.reshape(group_count, block_rows * slots, total_rows), axis=1)
    named = union * (owner[None, :] != groups[:, None]).astype(jnp.int32)
    by_owner = named.reshape(group_count, group_count, block_rows)
    row_rank = (jnp.cumsum(by_owner, axis=2) - by_owner).reshape(group_count, total_rows)
    useful = jnp.max(union[:, None, None, :] * hits[None], axis=3)
    slot_rank = jnp.cumsum(useful, axis=2) - useful
    to_group = (group_index + 1 + jnp.arange(offsets, dtype=jnp.int32)) % group_count
    locals_ = jnp.arange(block_rows, dtype=jnp.int32)
    named_here = lax.dynamic_slice_in_dim(named, first_row, block_rows, 1)[to_group]
    rank_here = lax.dynamic_slice_in_dim(row_rank, first_row, block_rows, 1)[to_group]
    caps = jnp.arange(CAPX, dtype=jnp.int32)
    chosen = named_here[:, None, :] * (rank_here[:, None, :] == caps[None, :, None])
    send_row = jnp.sum(chosen * locals_, axis=2).astype(jnp.int32)
    useful_here = lax.dynamic_slice_in_dim(useful, first_row, block_rows, 1)[to_group]
    srank_here = lax.dynamic_slice_in_dim(slot_rank, first_row, block_rows, 1)[to_group]
    cap_ids = jnp.arange(cap_slots, dtype=jnp.int32)
    slot_ids = jnp.arange(slots, dtype=jnp.int32)
    picks = useful_here[:, :, None, :] * (
        srank_here[:, :, None, :] == cap_ids[None, None, :, None]
    )
    slot_of = jnp.sum(picks * slot_ids, axis=3)
    send_slot = jnp.sum(chosen[:, :, :, None] * slot_of[:, None, :, :], axis=2).astype(jnp.int32)
    my_rank = lax.dynamic_index_in_dim(row_rank, group_index, 0, keepdims=False)
    my_slot_rank = lax.dynamic_index_in_dim(slot_rank, group_index, 0, keepdims=False)
    distance = (group_index - owner) % group_count
    is_local = distance == 0
    row_source = jnp.where(is_local, targets - first_row, block_rows + distance - 1)
    node_place = jnp.where(
        is_local, targets - first_row, block_rows + (distance - 1) * CAPX + my_rank
    )
    own_cols = lax.dynamic_slice_in_dim(block_cols, first_row, block_rows, 0)
    near_cols = block_cols[own_cols]
    match = near_cols[:, :, None, :] == own_cols[:, None, :, None]
    found = jnp.max(match.astype(jnp.int32), axis=3)
    slot_place = jnp.where(
        is_local[:, None], slot_ids[None, :], my_rank[:, None] * cap_slots + my_slot_rank
    )
    place = jnp.sum(match.astype(jnp.int32) * slot_place[own_cols][:, :, None, :], axis=3)
    tri_place = jnp.where(found > 0, place, -1).astype(jnp.int32)
    tri_source = row_source[own_cols].astype(jnp.int32)
    return (send_row, send_slot, own_cols, tri_source, tri_place, node_place.astype(jnp.int32))


def per_device(
    pair_feats,
    block_cols,
    attn_mask,
    chain_of_row,
    same_chain,
    node_feats,
    node_cotangent,
    tri_weight,
    gate_weight,
    tri_out_weight,
    bias_weight,
    query_weight,
    key_weight,
    value_weight,
    out_weight,
):
    parts = lax.axis_size("row")
    group_count = lax.axis_size("grp")
    group_index = lax.axis_index("grp")
    row_index = lax.axis_index("row")
    block_rows, slots, rows, block, channels = pair_feats.shape
    hidden = tri_weight.shape[1] // 4
    heads = bias_weight.shape[1]
    width = node_feats.shape[1]
    offsets = group_count - 1
    first_row = group_index * block_rows
    send_row, send_slot, own_cols, tri_source, tri_place, node_place = make_plan(
        block_cols, group_index, group_count, block_rows
    )
    rings = [
        [(g, (g + d) % group_count) for g in range(group_count)] for d in range(1, group_count)
    ]

    weights_t = jnp.concatenate([tri_weight.T * 0.5, bias_weight.T], axis=0).astype(BF16)
    own_weights = jnp.stack([query_weight.T, key_weight.T, value_weight.T, out_weight])
    share = own_weights.shape[0] * own_weights.shape[1] // group_count
    own_share = lax.dynamic_slice_in_dim(
        own_weights.reshape(-1, width), group_index * share, share, 0
    )
    row_steps = doubling_steps("row")
    near_share = doubled(own_share[None], "row", row_steps[:1])

    def swap(values, *earlier):
        return lax.all_to_all(
            after(values, *earlier), "row", split_axis=0, concat_axis=0, tiled=True
        )

    groups = [(0, LEAD), (LEAD, block_rows - LEAD)]
    left_near_0, left_0, right_near_0, right_0, bias_0 = project_rows(
        pair_feats, weights_t, parts, *groups[0], heads
    )
    right_near_0 = swap(right_near_0, near_share)
    left_near_1, left_1, right_near_1, right_1, bias_1 = project_rows(
        pair_feats, weights_t, parts, *groups[1], heads
    )
    biases = (bias_0, bias_1)
    half_share = doubled(near_share, "row", row_steps[1:-1])
    right_near_1 = swap(right_near_1, right_near_0, half_share)
    rights_near = [right_near_0, right_near_1]
    row_share = doubled(half_share, "row", row_steps[-1:])
    all_stack = jnp.swapaxes(doubled(row_share[None], "grp", doubling_steps("grp")), 0, 1)
    row_order, grp_order = doubled_order("row"), doubled_order("grp")
    plan_parts = (send_row, send_slot, node_place, tri_source, tri_place)
    span = parts // 2
    half_place = row_index % span

    def pairwise(pieces):
        return [pieces[0]] + [
            lax.ppermute(pieces[d], "row", [(r, r ^ d) for r in range(parts)])
            for d in range(1, span)
        ]

    def pieces_of(stacked):
        return [
            lax.dynamic_slice_in_dim(stacked, half_place ^ d, 1, 0) for d in range(span)
        ]

    left_near_1 = pairwise(pieces_of(left_near_1))
    left_near_0 = pairwise(pieces_of(left_near_0))
    right_all = swap(
        jnp.concatenate([right_0, right_1], axis=1), right_near_1, all_stack, *plan_parts, *left_near_0, *left_near_1
    )
    rights = [right_all]
    outgoing_near = pick_blocks(rights_near, send_row, send_slot, offsets)
    arrived_near = [lax.ppermute(v, "grp", ring) for v, ring in zip(outgoing_near, rings)]
    all_stack = after(all_stack, *outgoing_near)

    all_weights = all_stack[row_order[:, None], grp_order[None, :]].reshape(
        (parts,) + own_weights.shape
    )

    def full(number):
        return all_weights[:, number].reshape(width, width)

    node_norm = norm_parts(node_feats.astype(F32), 1)[0].astype(BF16)
    norm_blocks = node_norm.reshape(block_rows, block, width)
    far_nodes = [
        lax.ppermute(norm_blocks[send_row[d]], "grp", rings[d]) for d in range(offsets)
    ]
    near_nodes = jnp.concatenate([norm_blocks] + far_nodes, axis=0).reshape(-1, width)

    def times_t(values, weight):
        return lax.dot_general(
            values, weight, (((1,), (1,)), ((), ())), preferred_element_type=F32
        ).astype(BF16)

    keys = times_t(near_nodes, full(1)).reshape(-1, block, width)
    values = times_t(near_nodes, full(2)).reshape(-1, block, width)

    def own_rows(array):
        return lax.dynamic_slice_in_dim(
            array.reshape(block_rows, block, width), row_index * rows, rows, 1
        ).reshape(block_rows * rows, width)

    queries = times_t(own_rows(node_norm), full(0)).reshape(block_rows, rows, width)
    cots = times_t(own_rows(node_cotangent), full(3)).reshape(block_rows, rows, width)
    own_chain = lax.dynamic_slice_in_dim(chain_of_row, first_row, block_rows, 0)
    masks = lax.dynamic_slice_in_dim(attn_mask, first_row, block_rows, 0)
    flags = (chain_of_row[own_cols] == own_chain[:, None]).astype(F32)
    chain_bias = jnp.broadcast_to(same_chain[:, None], (heads, block))
    mixed, grads = attend(
        queries,
        cots,
        keys,
        values,
        biases,
        node_place[own_cols],
        masks,
        flags,
        chain_bias,
        arrived_near[0],
    )

    bias_float = bias_weight.astype(F32)
    centred = (bias_float - jnp.mean(bias_float, axis=0, keepdims=True)).T
    zeros = jnp.zeros((heads, channels), F32)
    back_weight = jnp.concatenate(
        [
            jnp.concatenate([centred, zeros], axis=1),
            jnp.concatenate([zeros, zeros + 1.0 / heads], axis=1),
        ],
        axis=0,
    ).astype(BF16)
    gate_half = (gate_weight * 0.5).astype(BF16)
    whole = ()
    for (first, _), bias in zip(groups, biases):
        whole = gradient_rows(
            pair_feats, grads, bias, gate_half, back_weight, heads, first, whole
        )
    pair_out, pair_grad = whole

    left_rest = swap(left_1, right_all)
    outgoing = pick_blocks(rights, send_row, send_slot, offsets)
    arrived = [lax.ppermute(v, "grp", ring) for v, ring in zip(outgoing, rings)]
    near_mixed, first_mixed = mixed[None], None
    for step in [1 << n for n in range(block_rows.bit_length() - 1)]:
        other = lax.ppermute(near_mixed, "row", [(r, r ^ step) for r in range(parts)])
        swapped = (row_index & step) > 0
        near_mixed = jnp.concatenate(
            [jnp.where(swapped, other, near_mixed), jnp.where(swapped, near_mixed, other)], axis=0
        )
        first_mixed = near_mixed if first_mixed is None else first_mixed
    left_lead = swap(left_0, left_rest, first_mixed, pair_grad, *outgoing)
    sharers = parts // block_rows
    sent_mixed = lax.dynamic_index_in_dim(near_mixed, row_index % block_rows, 1, keepdims=False)
    senders = [((r % sharers) * block_rows + r // sharers, r) for r in range(parts)]
    node_rows = block_rows * block // parts
    mixed_own = lax.ppermute(sent_mixed, "row", senders).reshape(node_rows, width)
    near_args = (rights_near, arrived_near, tri_source, tri_place)
    args = (rights, arrived, tri_source, tri_place)
    near_sums_1 = triangle_rows(left_near_1, *near_args, LEAD, pair_grad, *outgoing)
    near_rest = pairwise(near_sums_1)
    sums = triangle_rows([left_rest], *args, LEAD, near_sums_1[0])[0]
    tri_rest = swap(sums, left_lead)
    near_sums_0 = triangle_rows(left_near_0, *near_args, 0, sums)
    near_lead = pairwise(near_sums_0)
    sums = triangle_rows([left_lead], *args, 0, near_sums_0[0], mixed_own)[0]
    tri_lead = swap(sums, tri_rest)
    own_nodes = lax.dynamic_slice_in_dim(node_feats, row_index * node_rows, node_rows, 0)
    node_out = (
        own_nodes.astype(F32) + jnp.dot(mixed_own, full(3), preferred_element_type=F32)
    ).astype(BF16)
    tri_lead = after(tri_lead, node_out)
    place = half_place.reshape(1).astype(jnp.int32)
    pair_out = finish_rows(
        pair_feats, pair_out, near_rest, tri_rest, tri_out_weight, place, LEAD
    )
    pair_out = finish_rows(pair_feats, pair_out, near_lead, tri_lead, tri_out_weight, place, 0)
    return (pair_out, node_out, pair_grad)


def solution(mesh):
    pair_spec = P("grp", None, "row", None, None)
    in_specs = (
        (pair_spec,)
        + (P(),) * 4
        + (P("grp", None),) * 2
        + (P(),) * 4
        + (P(None, "row"),) * 3
        + (P("row", None),)
    )
    out_specs = (pair_spec, P(("grp", "row"), None), pair_spec)
    return jax.shard_map(
        per_device, mesh=mesh, in_specs=in_specs, out_specs=out_specs, check_vma=False
    )
```

```python
import jax
import jax.numpy as jnp
from jax import lax
from jax.experimental import pallas as pl
from jax.experimental.pallas import tpu as pltpu
from jax.sharding import PartitionSpec as P

CAPX = 2
LEAD = 1
EPS = 1e-05
F32 = jnp.float32
BF16 = jnp.bfloat16
VMEM_BYTES = 56 * 1024 * 1024


def norm_parts(values, dimension):
    center = jnp.mean(values, axis=dimension, keepdims=True)
    shifted = values - center
    spread = jnp.mean(shifted * shifted, axis=dimension, keepdims=True)
    inverse = lax.rsqrt(spread + EPS)
    return (shifted * inverse, inverse)


def chunk_starts(chunks, dimension):
    spans, start = [], 0
    for chunk in chunks:
        spans.append((start, start + chunk.shape[dimension]))
        start = spans[-1][1]
    return spans


def params():
    return pltpu.CompilerParams(vmem_limit_bytes=VMEM_BYTES)


def project_rows(pair_feats, weights_t, parts, first, count, heads):
    slots, rows, block, channels = pair_feats.shape[1:]
    hidden = (weights_t.shape[0] - heads) // 4
    part = hidden // parts
    step_rows = 2

    def body(x_ref, w_ref, left_ref, right_ref, bias_ref, left_buf, right_buf):
        weights = w_ref[...]
        for start in range(0, rows, step_rows):
            x = x_ref[start : start + step_rows].astype(F32).reshape(step_rows * block, channels)
            normed = norm_parts(x, 1)[0].astype(BF16)
            projected = lax.dot_general(
                weights, normed, (((1,), (1,)), ((), ())), preferred_element_type=F32
            )
            left_half = projected[:hidden]
            left = left_half * jnp.tanh(projected[hidden : 2 * hidden]) + left_half
            right_half = projected[2 * hidden : 3 * hidden]
            right = right_half * jnp.tanh(projected[3 * hidden : 4 * hidden]) + right_half
            bias = projected[4 * hidden :].astype(BF16)
            for inner in range(step_rows):
                lanes = slice(inner * block, (inner + 1) * block)
                place = start + inner
                left_buf[:, place, :] = left[:, lanes]
                right_buf[:, place, :] = right[:, lanes]
                bias_ref[place * heads : (place + 1) * heads, :] = bias[:, lanes]
        shape = (parts, part, rows, block)
        left_ref[...] = left_buf[...].astype(BF16).reshape(shape)
        right_ref[...] = right_buf[...].astype(BF16).reshape(shape)

    shipped = jax.ShapeDtypeStruct((parts, count, slots, part, rows, block), BF16)
    shipped_spec = pl.BlockSpec(
        (parts, None, None, part, rows, block), lambda i, s: (0, i, s, 0, 0, 0)
    )
    return pl.pallas_call(
        body,
        grid=(count, slots),
        in_specs=[
            pl.BlockSpec((None, None, rows, block, channels), lambda i, s: (first + i, s, 0, 0, 0)),
            pl.BlockSpec(weights_t.shape, lambda i, s: (0, 0)),
        ],
        out_specs=[
            shipped_spec,
            shipped_spec,
            pl.BlockSpec((None, None, rows * heads, block), lambda i, s: (i, s, 0, 0)),
        ],
        out_shape=[
            shipped,
            shipped,
            jax.ShapeDtypeStruct((count, slots, rows * heads, block), BF16),
        ],
        scratch_shapes=[pltpu.VMEM((hidden, rows, block), F32)] * 2,
        compiler_params=params(),
        name=f"project_{first}",
    )(pair_feats, weights_t)


def pick_blocks(rights, send_row, send_slot, offsets):
    parts, _, _, part, rows, block = rights[0].shape
    _, cap_rows, cap_slots = send_slot.shape
    starts = chunk_starts(rights, 1)

    def body(row_ref, slot_ref, *refs):
        ins, out_refs = refs[: len(rights)], refs[len(rights) :]
        for offset in range(offsets):
            for a in range(cap_rows):
                which = row_ref[offset, a]
                for chunk, (begin, end) in enumerate(starts):

                    @pl.when((which >= begin) & (which < end))
                    def _(chunk=chunk, begin=begin, a=a, offset=offset, which=which):
                        for b in range(cap_slots):
                            slot = slot_ref[offset, a, b]
                            for d in range(parts):
                                out_refs[offset][a * cap_slots + b, d] = ins[chunk][
                                    d, which - begin, slot
                                ]

    out = jax.ShapeDtypeStruct((cap_rows * cap_slots, parts, part, rows, block), BF16)
    smem = pl.BlockSpec(memory_space=pltpu.SMEM)
    vmem = pl.BlockSpec(memory_space=pltpu.VMEM)
    return pl.pallas_call(
        body,
        in_specs=[smem, smem] + [vmem] * len(rights),
        out_specs=[vmem] * offsets,
        out_shape=[out] * offsets,
        compiler_params=params(),
        name="pick_blocks",
    )(send_row, send_slot, *rights)


def triangle_rows(left, rights, arrived, source, place, first, *earlier):
    far = len(arrived)
    parts, count, slots, part, rows, block = left.shape
    starts = chunk_starts(rights, 1)
    held = BF16 if rows % 16 == 0 else F32

    def body(source_ref, place_ref, left_ref, *refs):
        right_refs, refs = refs[: len(rights)], refs[len(rights) :]
        far_refs, (out_ref, table) = refs[:far], refs[far + len(earlier) :]
        at_row = first + pl.program_id(1)
        for s in range(slots):
            origin = source_ref[at_row, s]

            def fill(get, s=s):
                for t in range(slots):
                    there = slice(t * block, (t + 1) * block)
                    at = place_ref[at_row, s, t]

                    @pl.when(at >= 0)
                    def _():
                        for d in range(parts):
                            begin = s * block + d * rows
                            table[begin : begin + rows, there] = get(d, at).astype(held)

                    @pl.when(at < 0)
                    def _():
                        table[s * block : (s + 1) * block, there] = jnp.zeros((block, block), held)

            for chunk, (begin, end) in enumerate(starts):

                @pl.when((origin >= begin) & (origin < end))
                def _(chunk=chunk, begin=begin):
                    fill(lambda d, at: right_refs[chunk][d, origin - begin, at])

            for number in range(far):

                @pl.when(origin == starts[-1][1] + number)
                def _(number=number):
                    fill(lambda d, at: far_refs[number][at, d])

        near = jnp.concatenate(
            [
                jnp.concatenate([left_ref[d, t].astype(held) for d in range(parts)], axis=0)
                for t in range(slots)
            ],
            axis=1,
        ).astype(BF16)
        sums = lax.dot_general(
            near,
            table[...].astype(BF16),
            (((1,), (1,)), ((), ())),
            preferred_element_type=F32,
        )
        for d in range(parts):
            for s in range(slots):
                piece = sums[d * rows : (d + 1) * rows, s * block : (s + 1) * block]
                out_ref[d, s] = piece.astype(BF16)

    smem = pl.BlockSpec(memory_space=pltpu.SMEM)
    row_spec = pl.BlockSpec(
        (parts, None, slots, None, rows, block), lambda c, i: (0, i, 0, c, 0, 0)
    )
    far_spec = pl.BlockSpec(
        arrived[0].shape[:2] + (None, rows, block), lambda c, i: (0, 0, c, 0, 0)
    )
    return pl.pallas_call(
        body,
        grid=(part, count),
        in_specs=[smem] * 2
        + [row_spec]
        + [
            pl.BlockSpec(right.shape[:3] + (None, rows, block), lambda c, i: (0, 0, 0, c, 0, 0))
            for right in rights
        ]
        + [far_spec] * far
        + [pl.BlockSpec(memory_space=pl.ANY)] * len(earlier),
        out_specs=row_spec,
        out_shape=jax.ShapeDtypeStruct(left.shape, BF16),
        scratch_shapes=[pltpu.VMEM((slots * block, slots * block), held)],
        compiler_params=params(),
        name=f"triangle_{first}",
    )(source, place, left, *rights, *arrived, *earlier)


def attend(queries, cots, keys, values, bias_rows, places, masks, flags, chain_bias):
    block_rows, rows, width = queries.shape
    heads = chain_bias.shape[0]
    _, slots, _, block = bias_rows[0].shape
    chunks = len(bias_rows)
    chunk_of = [
        (chunk, I - begin)
        for chunk, (begin, end) in enumerate(chunk_starts(bias_rows, 0))
        for I in range(begin, end)
    ]
    head_size = width // heads
    score_scale = head_size ** (-0.5)

    def body(place_ref, mask_ref, flag_ref, q_ref, c_ref, k_ref, v_ref, chain_ref, *refs):
        bias_refs, (mixed_ref, grad_ref) = refs[:chunks], refs[chunks:]
        row_head = lax.broadcasted_iota(jnp.int32, (heads, width), 0)
        lane_head = lax.broadcasted_iota(jnp.int32, (heads, width), 1) // head_size
        own_head = (row_head == lane_head).astype(F32)
        chain = jnp.concatenate([chain_ref[...]] * rows, axis=0)
        for I, (chunk, inner) in enumerate(chunk_of):

            def spread(ref):
                wide = ref[I].astype(F32)
                return jnp.concatenate(
                    [
                        (jnp.broadcast_to(wide[i : i + 1], (heads, width)) * own_head).astype(BF16)
                        for i in range(rows)
                    ],
                    axis=0,
                )

            q_wide, c_wide = spread(q_ref), spread(c_ref)
            scores, grads = [], []
            for s in range(slots):
                near = place_ref[I, s]
                score = lax.dot_general(
                    q_wide, k_ref[near], (((1,), (1,)), ((), ())), preferred_element_type=F32
                )
                score = score * score_scale + bias_refs[chunk][inner, s].astype(F32) + chain * flag_ref[I, s]
                scores.append(jnp.where(mask_ref[I, s] > 0, score, -jnp.inf))
                grads.append(
                    lax.dot_general(
                        c_wide, v_ref[near], (((1,), (1,)), ((), ())), preferred_element_type=F32
                    )
                )
            scores = jnp.concatenate(scores, axis=1)
            grads = jnp.concatenate(grads, axis=1)
            exps = jnp.exp(scores - jnp.max(scores, axis=1, keepdims=True))
            probs = exps / jnp.sum(exps, axis=1, keepdims=True)
            low = probs.astype(BF16)
            mixed = jnp.zeros((rows * heads, width), F32)
            for s in range(slots):
                mixed = mixed + jnp.dot(
                    low[:, s * block : (s + 1) * block],
                    v_ref[place_ref[I, s]],
                    preferred_element_type=F32,
                )
            mixed = mixed.reshape(rows, heads, width) * own_head[None]
            mixed_ref[I] = jnp.sum(mixed, axis=1).astype(BF16)
            total = jnp.sum(probs * grads, axis=1, keepdims=True)
            score_grads = (probs * (grads - total)).astype(BF16)
            for s in range(slots):
                grad_ref[I, s] = score_grads[:, s * block : (s + 1) * block]

    smem = pl.BlockSpec(memory_space=pltpu.SMEM)
    vmem = pl.BlockSpec(memory_space=pltpu.VMEM)
    return pl.pallas_call(
        body,
        in_specs=[smem] * 3 + [vmem] * (5 + chunks),
        out_specs=[vmem, vmem],
        out_shape=[
            jax.ShapeDtypeStruct((block_rows, rows, width), BF16),
            jax.ShapeDtypeStruct((block_rows, slots, rows * heads, block), BF16),
        ],
        compiler_params=params(),
        name="attend",
    )(places, masks, flags, queries, cots, keys, values, chain_bias, *bias_rows)


def gradient_rows(pair_feats, grads, bias_rows, gate_half, back_weight, heads, first, earlier):
    count = bias_rows.shape[0]
    slots, rows, block, channels = pair_feats.shape[1:]

    def body(x_ref, g_ref, b_ref, gate_ref, back_ref, *refs):
        out_ref, grad_ref = refs[-2:]
        gate_weight, back = gate_ref[...], back_ref[...]
        for i in range(rows):
            xhat, scale = norm_parts(x_ref[i].astype(F32), 1)
            gate = jnp.dot(xhat.astype(BF16), gate_weight, preferred_element_type=F32)
            out_ref[i] = (0.5 * jnp.tanh(gate) + 0.5).astype(BF16)
            g = g_ref[i * heads : (i + 1) * heads]
            b = b_ref[i * heads : (i + 1) * heads]
            cross = jnp.sum(g.astype(F32) * b.astype(F32), axis=0, keepdims=True) / channels
            cross = jnp.broadcast_to(cross, (heads, block)).astype(BF16)
            both = lax.dot_general(
                jnp.concatenate([g, cross], axis=0),
                back,
                (((0,), (0,)), ((), ())),
                preferred_element_type=F32,
            )
            centred, projection = both[:, :channels], both[:, channels:]
            grad_ref[i] = (scale * (centred - xhat * projection)).astype(BF16)

    big = pl.BlockSpec((None, None, rows, block, channels), lambda i, s: (first + i, s, 0, 0, 0))
    whole = jax.ShapeDtypeStruct(pair_feats.shape, BF16)
    anywhere = pl.BlockSpec(memory_space=pl.ANY)
    return pl.pallas_call(
        body,
        grid=(count, slots),
        in_specs=[
            big,
            pl.BlockSpec((None, None, rows * heads, block), lambda i, s: (first + i, s, 0, 0)),
            pl.BlockSpec((None, None, rows * heads, block), lambda i, s: (i, s, 0, 0)),
            pl.BlockSpec(gate_half.shape, lambda i, s: (0, 0)),
            pl.BlockSpec(back_weight.shape, lambda i, s: (0, 0)),
        ]
        + [anywhere] * len(earlier),
        out_specs=[big, big],
        out_shape=[whole, whole],
        input_output_aliases={5 + n: n for n in range(len(earlier))},
        compiler_params=params(),
        name=f"gradient_{first}",
    )(pair_feats, grads, bias_rows, gate_half, back_weight, *earlier)


def finish_rows(pair_feats, gates, tri, tri_out_weight, first):
    slots, rows, block, channels = pair_feats.shape[1:]
    parts, count, _, part, _, _ = tri.shape
    hidden = parts * part

    def body(x_ref, gate_ref, tri_ref, w_ref, out_ref, buf):
        sums = tri_ref[...].astype(F32).reshape(hidden, rows, block)
        buf[...] = norm_parts(sums, 0)[0]
        weight = w_ref[...]
        for i in range(rows):
            update = lax.dot_general(
                buf[:, i, :].astype(BF16),
                weight,
                (((0,), (0,)), ((), ())),
                preferred_element_type=F32,
            )
            out_ref[i] = (x_ref[i].astype(F32) + gate_ref[i].astype(F32) * update).astype(BF16)

    big = pl.BlockSpec((None, None, rows, block, channels), lambda i, s: (first + i, s, 0, 0, 0))
    return pl.pallas_call(
        body,
        grid=(count, slots),
        in_specs=[
            big,
            big,
            pl.BlockSpec(
                (parts, None, None, part, rows, block), lambda i, s: (0, i, s, 0, 0, 0)
            ),
            pl.BlockSpec(tri_out_weight.shape, lambda i, s: (0, 0)),
        ],
        out_specs=big,
        out_shape=jax.ShapeDtypeStruct(pair_feats.shape, BF16),
        input_output_aliases={1: 0},
        scratch_shapes=[pltpu.VMEM((hidden, rows, block), F32)],
        compiler_params=params(),
        name=f"finish_{first}",
    )(pair_feats, gates, tri, tri_out_weight)


def after(values, *earlier):
    return lax.optimization_barrier((values,) + earlier)[0]


def doubling_steps(axis):
    size = lax.axis_size(axis)
    return [size >> n for n in range(1, size.bit_length())]


def doubled(stacked, axis, steps):
    size = lax.axis_size(axis)
    for step in steps:
        pairs = [(n, n ^ step) for n in range(size)]
        stacked = jnp.concatenate([stacked, lax.ppermute(stacked, axis, pairs)], axis=0)
    return stacked


def doubled_order(axis):
    away = jnp.arange(lax.axis_size(axis), dtype=jnp.int32) ^ lax.axis_index(axis)
    order = jnp.zeros_like(away)
    for number, step in enumerate(doubling_steps(axis)):
        order = order + jnp.where(away & step, 1 << number, 0)
    return order


def make_plan(block_cols, group_index, group_count, block_rows):
    total_rows, slots = block_cols.shape
    offsets = group_count - 1
    cap_slots = slots - block_rows + CAPX
    first_row = group_index * block_rows
    targets = jnp.arange(total_rows, dtype=jnp.int32)
    owner = targets // block_rows
    groups = jnp.arange(group_count, dtype=jnp.int32)
    hits = (block_cols[:, :, None] == targets).astype(jnp.int32)
    union = jnp.max(hits.reshape(group_count, block_rows * slots, total_rows), axis=1)
    named = union * (owner[None, :] != groups[:, None]).astype(jnp.int32)
    by_owner = named.reshape(group_count, group_count, block_rows)
    row_rank = (jnp.cumsum(by_owner, axis=2) - by_owner).reshape(group_count, total_rows)
    useful = jnp.max(union[:, None, None, :] * hits[None], axis=3)
    slot_rank = jnp.cumsum(useful, axis=2) - useful
    to_group = (group_index + 1 + jnp.arange(offsets, dtype=jnp.int32)) % group_count
    locals_ = jnp.arange(block_rows, dtype=jnp.int32)
    named_here = lax.dynamic_slice_in_dim(named, first_row, block_rows, 1)[to_group]
    rank_here = lax.dynamic_slice_in_dim(row_rank, first_row, block_rows, 1)[to_group]
    caps = jnp.arange(CAPX, dtype=jnp.int32)
    chosen = named_here[:, None, :] * (rank_here[:, None, :] == caps[None, :, None])
    send_row = jnp.sum(chosen * locals_, axis=2).astype(jnp.int32)
    useful_here = lax.dynamic_slice_in_dim(useful, first_row, block_rows, 1)[to_group]
    srank_here = lax.dynamic_slice_in_dim(slot_rank, first_row, block_rows, 1)[to_group]
    cap_ids = jnp.arange(cap_slots, dtype=jnp.int32)
    slot_ids = jnp.arange(slots, dtype=jnp.int32)
    picks = useful_here[:, :, None, :] * (
        srank_here[:, :, None, :] == cap_ids[None, None, :, None]
    )
    slot_of = jnp.sum(picks * slot_ids, axis=3)
    send_slot = jnp.sum(chosen[:, :, :, None] * slot_of[:, None, :, :], axis=2).astype(jnp.int32)
    my_rank = lax.dynamic_index_in_dim(row_rank, group_index, 0, keepdims=False)
    my_slot_rank = lax.dynamic_index_in_dim(slot_rank, group_index, 0, keepdims=False)
    distance = (group_index - owner) % group_count
    is_local = distance == 0
    row_source = jnp.where(is_local, targets - first_row, block_rows + distance - 1)
    node_place = jnp.where(
        is_local, targets - first_row, block_rows + (distance - 1) * CAPX + my_rank
    )
    own_cols = lax.dynamic_slice_in_dim(block_cols, first_row, block_rows, 0)
    near_cols = block_cols[own_cols]
    match = near_cols[:, :, None, :] == own_cols[:, None, :, None]
    found = jnp.max(match.astype(jnp.int32), axis=3)
    slot_place = jnp.where(
        is_local[:, None], slot_ids[None, :], my_rank[:, None] * cap_slots + my_slot_rank
    )
    place = jnp.sum(match.astype(jnp.int32) * slot_place[own_cols][:, :, None, :], axis=3)
    tri_place = jnp.where(found > 0, place, -1).astype(jnp.int32)
    tri_source = row_source[own_cols].astype(jnp.int32)
    return (send_row, send_slot, own_cols, tri_source, tri_place, node_place.astype(jnp.int32))


def per_device(
    pair_feats,
    block_cols,
    attn_mask,
    chain_of_row,
    same_chain,
    node_feats,
    node_cotangent,
    tri_weight,
    gate_weight,
    tri_out_weight,
    bias_weight,
    query_weight,
    key_weight,
    value_weight,
    out_weight,
):
    parts = lax.axis_size("row")
    group_count = lax.axis_size("grp")
    group_index = lax.axis_index("grp")
    row_index = lax.axis_index("row")
    block_rows, slots, rows, block, channels = pair_feats.shape
    hidden = tri_weight.shape[1] // 4
    heads = bias_weight.shape[1]
    width = node_feats.shape[1]
    offsets = group_count - 1
    first_row = group_index * block_rows
    send_row, send_slot, own_cols, tri_source, tri_place, node_place = make_plan(
        block_cols, group_index, group_count, block_rows
    )
    rings = [
        [(g, (g + d) % group_count) for g in range(group_count)] for d in range(1, group_count)
    ]

    weights_t = jnp.concatenate([tri_weight.T * 0.5, bias_weight.T], axis=0).astype(BF16)
    own_weights = jnp.stack([query_weight.T, key_weight.T, value_weight.T, out_weight])
    share = own_weights.shape[0] * own_weights.shape[1] // group_count
    own_share = lax.dynamic_slice_in_dim(
        own_weights.reshape(-1, width), group_index * share, share, 0
    )
    row_steps = doubling_steps("row")
    near_share = doubled(own_share[None], "row", row_steps[:1])

    def swap(values, *earlier):
        return lax.all_to_all(
            after(values, *earlier), "row", split_axis=0, concat_axis=0, tiled=True
        )

    groups = [(0, LEAD), (LEAD, block_rows - LEAD)]
    left_0, right_0, bias_0 = project_rows(pair_feats, weights_t, parts, *groups[0], heads)
    right_lead = swap(right_0, near_share)
    left_1, right_1, bias_1 = project_rows(pair_feats, weights_t, parts, *groups[1], heads)
    lefts, rights, biases = (left_0, left_1), (right_0, right_1), (bias_0, bias_1)
    half_share = doubled(near_share, "row", row_steps[1:-1])
    right_rest = swap(rights[1], right_lead, half_share)
    row_share = doubled(half_share, "row", row_steps[-1:])
    all_stack = jnp.swapaxes(doubled(row_share[None], "grp", doubling_steps("grp")), 0, 1)
    row_order, grp_order = doubled_order("row"), doubled_order("grp")
    rights = [right_lead, right_rest]
    left_rest = swap(
        lefts[1], right_rest, all_stack, send_row, send_slot, node_place, tri_source, tri_place
    )
    outgoing = pick_blocks(rights, send_row, send_slot, offsets)
    arrived = [lax.ppermute(v, "grp", ring) for v, ring in zip(outgoing, rings)]
    all_stack = after(all_stack, *outgoing)

    all_weights = all_stack[row_order[:, None], grp_order[None, :]].reshape(
        (parts,) + own_weights.shape
    )

    def full(number):
        return all_weights[:, number].reshape(width, width)

    node_norm = norm_parts(node_feats.astype(F32), 1)[0].astype(BF16)
    norm_blocks = node_norm.reshape(block_rows, block, width)
    far_nodes = [
        lax.ppermute(norm_blocks[send_row[d]], "grp", rings[d]) for d in range(offsets)
    ]
    near_nodes = jnp.concatenate([norm_blocks] + far_nodes, axis=0).reshape(-1, width)

    def times_t(values, weight):
        return lax.dot_general(
            values, weight, (((1,), (1,)), ((), ())), preferred_element_type=F32
        ).astype(BF16)

    keys = times_t(near_nodes, full(1)).reshape(-1, block, width)
    values = times_t(near_nodes, full(2)).reshape(-1, block, width)

    def own_rows(array):
        return lax.dynamic_slice_in_dim(
            array.reshape(block_rows, block, width), row_index * rows, rows, 1
        ).reshape(block_rows * rows, width)

    queries = times_t(own_rows(node_norm), full(0)).reshape(block_rows, rows, width)
    cots = times_t(own_rows(node_cotangent), full(3)).reshape(block_rows, rows, width)
    own_chain = lax.dynamic_slice_in_dim(chain_of_row, first_row, block_rows, 0)
    masks = lax.dynamic_slice_in_dim(attn_mask, first_row, block_rows, 0)
    flags = (chain_of_row[own_cols] == own_chain[:, None]).astype(F32)
    chain_bias = jnp.broadcast_to(same_chain[:, None], (heads, block))
    mixed, grads = attend(
        queries, cots, keys, values, biases, node_place[own_cols], masks, flags, chain_bias
    )
    bias_float = bias_weight.astype(F32)
    centred = (bias_float - jnp.mean(bias_float, axis=0, keepdims=True)).T
    zeros = jnp.zeros((heads, channels), F32)
    back_weight = jnp.concatenate(
        [
            jnp.concatenate([centred, zeros], axis=1),
            jnp.concatenate([zeros, zeros + 1.0 / heads], axis=1),
        ],
        axis=0,
    ).astype(BF16)
    gate_half = (gate_weight * 0.5).astype(BF16)
    whole = ()
    for (first, _), bias in zip(groups, biases):
        whole = gradient_rows(
            pair_feats, grads, bias, gate_half, back_weight, heads, first, whole
        )
    pair_out, pair_grad = whole

    near_mixed = mixed[None]
    for step in [1 << n for n in range(block_rows.bit_length() - 1)]:
        other = lax.ppermute(near_mixed, "row", [(r, r ^ step) for r in range(parts)])
        swapped = (row_index & step) > 0
        near_mixed = jnp.concatenate(
            [jnp.where(swapped, other, near_mixed), jnp.where(swapped, near_mixed, other)], axis=0
        )
    left_lead = swap(lefts[0], left_rest, near_mixed, pair_grad, *arrived)
    sums = triangle_rows(left_rest, rights, arrived, tri_source, tri_place, LEAD)
    tri_rest = swap(sums, left_lead)
    sharers = parts // block_rows
    sent_mixed = lax.dynamic_index_in_dim(near_mixed, row_index % block_rows, 1, keepdims=False)
    senders = [((r % sharers) * block_rows + r // sharers, r) for r in range(parts)]
    node_rows = block_rows * block // parts
    mixed_own = lax.ppermute(sent_mixed, "row", senders).reshape(node_rows, width)
    sums = triangle_rows(left_lead, rights, arrived, tri_source, tri_place, 0, mixed_own)
    tri_lead = swap(sums, tri_rest)
    own_nodes = lax.dynamic_slice_in_dim(node_feats, row_index * node_rows, node_rows, 0)
    node_out = (
        own_nodes.astype(F32) + jnp.dot(mixed_own, full(3), preferred_element_type=F32)
    ).astype(BF16)
    tri_lead = after(tri_lead, node_out)
    pair_out = finish_rows(pair_feats, pair_out, tri_rest, tri_out_weight, LEAD)
    pair_out = finish_rows(pair_feats, pair_out, tri_lead, tri_out_weight, 0)
    return (pair_out, node_out, pair_grad)


def solution(mesh):
    pair_spec = P("grp", None, "row", None, None)
    in_specs = (
        (pair_spec,)
        + (P(),) * 4
        + (P("grp", None),) * 2
        + (P(),) * 4
        + (P(None, "row"),) * 3
        + (P("row", None),)
    )
    out_specs = (pair_spec, P(("grp", "row"), None), pair_spec)
    return jax.shard_map(
        per_device, mesh=mesh, in_specs=in_specs, out_specs=out_specs, check_vma=False
    )
```

```python
import jax
import jax.numpy as jnp
from jax import lax
from jax.experimental import pallas as pl
from jax.experimental.pallas import tpu as pltpu
from jax.sharding import PartitionSpec as P

CAPX = 2
LEAD = 1
EPS = 1e-05
F32 = jnp.float32
BF16 = jnp.bfloat16
VMEM_BYTES = 56 * 1024 * 1024


def norm_parts(values, dimension):
    center = jnp.mean(values, axis=dimension, keepdims=True)
    shifted = values - center
    spread = jnp.mean(shifted * shifted, axis=dimension, keepdims=True)
    inverse = lax.rsqrt(spread + EPS)
    return (shifted * inverse, inverse)


def chunk_starts(chunks, dimension):
    spans, start = [], 0
    for chunk in chunks:
        spans.append((start, start + chunk.shape[dimension]))
        start = spans[-1][1]
    return spans


def params():
    return pltpu.CompilerParams(vmem_limit_bytes=VMEM_BYTES)


def project_rows(pair_feats, weights_t, parts, first, count, heads):
    slots, rows, block, channels = pair_feats.shape[1:]
    hidden = (weights_t.shape[0] - heads) // 4
    span = parts // 2
    near, part = hidden // 2, hidden // 2 // parts
    near_part = near // span
    step_rows = 2

    def body(
        x_ref, w_ref, left_near, left_ref, right_near, right_ref, bias_ref, left_buf, right_buf
    ):
        weights = w_ref[...]
        for start in range(0, rows, step_rows):
            x = x_ref[start : start + step_rows].astype(F32).reshape(step_rows * block, channels)
            normed = norm_parts(x, 1)[0].astype(BF16)
            projected = lax.dot_general(
                weights, normed, (((1,), (1,)), ((), ())), preferred_element_type=F32
            )
            left_half = projected[:hidden]
            left = left_half * jnp.tanh(projected[hidden : 2 * hidden]) + left_half
            right_half = projected[2 * hidden : 3 * hidden]
            right = right_half * jnp.tanh(projected[3 * hidden : 4 * hidden]) + right_half
            bias = projected[4 * hidden :].astype(BF16)
            for inner in range(step_rows):
                lanes = slice(inner * block, (inner + 1) * block)
                place = start + inner
                left_buf[:, place, :] = left[:, lanes]
                right_buf[:, place, :] = right[:, lanes]
                bias_ref[place * heads : (place + 1) * heads, :] = bias[:, lanes]
        shape, near_shape = (parts, part, rows, block), (span, near_part, rows, block)
        left_near[...] = left_buf[:near].astype(BF16).reshape(near_shape)
        left_ref[...] = left_buf[near:].astype(BF16).reshape(shape)
        right_half = right_buf[:near].astype(BF16).reshape(near_shape)
        right_near[:span] = right_half
        right_near[span:] = right_half
        right_ref[...] = right_buf[near:].astype(BF16).reshape(shape)

    shapes = [
        (devices, count, slots, channels_here, rows, block)
        for devices, channels_here in (
            (span, near_part),
            (parts, part),
            (parts, near_part),
            (parts, part),
        )
    ]
    return pl.pallas_call(
        body,
        grid=(count, slots),
        in_specs=[
            pl.BlockSpec((None, None, rows, block, channels), lambda i, s: (first + i, s, 0, 0, 0)),
            pl.BlockSpec(weights_t.shape, lambda i, s: (0, 0)),
        ],
        out_specs=[
            pl.BlockSpec(
                (shape[0], None, None) + shape[3:], lambda i, s: (0, i, s, 0, 0, 0)
            )
            for shape in shapes
        ]
        + [pl.BlockSpec((None, None, rows * heads, block), lambda i, s: (i, s, 0, 0))],
        out_shape=[jax.ShapeDtypeStruct(shape, BF16) for shape in shapes]
        + [jax.ShapeDtypeStruct((count, slots, rows * heads, block), BF16)],
        scratch_shapes=[pltpu.VMEM((hidden, rows, block), F32)] * 2,
        compiler_params=params(),
        name=f"project_{first}",
    )(pair_feats, weights_t)


def pick_blocks(rights, send_row, send_slot, offsets):
    parts, _, _, part, rows, block = rights[0].shape
    _, cap_rows, cap_slots = send_slot.shape
    starts = chunk_starts(rights, 1)

    def body(row_ref, slot_ref, *refs):
        ins, out_refs = refs[: len(rights)], refs[len(rights) :]
        for offset in range(offsets):
            for a in range(cap_rows):
                which = row_ref[offset, a]
                for chunk, (begin, end) in enumerate(starts):

                    @pl.when((which >= begin) & (which < end))
                    def _(chunk=chunk, begin=begin, a=a, offset=offset, which=which):
                        for b in range(cap_slots):
                            slot = slot_ref[offset, a, b]
                            for d in range(parts):
                                out_refs[offset][a * cap_slots + b, d] = ins[chunk][
                                    d, which - begin, slot
                                ]

    out = jax.ShapeDtypeStruct((cap_rows * cap_slots, parts, part, rows, block), BF16)
    smem = pl.BlockSpec(memory_space=pltpu.SMEM)
    vmem = pl.BlockSpec(memory_space=pltpu.VMEM)
    return pl.pallas_call(
        body,
        in_specs=[smem, smem] + [vmem] * len(rights),
        out_specs=[vmem] * offsets,
        out_shape=[out] * offsets,
        compiler_params=params(),
        name="pick_blocks",
    )(send_row, send_slot, *rights)


def triangle_rows(lefts, rights, arrived, source, place, first, *earlier):
    far, mine = len(arrived), len(lefts)
    parts = rights[0].shape[0]
    _, count, slots, part, rows, block = lefts[0].shape
    pieces = [(number, n) for number, left in enumerate(lefts) for n in range(left.shape[0])]
    starts = chunk_starts(rights, 1)
    held = BF16 if rows % 16 == 0 else F32

    def body(source_ref, place_ref, *refs):
        left_refs, refs = refs[:mine], refs[mine:]
        right_refs, refs = refs[: len(rights)], refs[len(rights) :]
        far_refs, refs = refs[:far], refs[far + len(earlier) :]
        out_refs, table = refs[:mine], refs[mine]
        at_row = first + pl.program_id(1)
        for s in range(slots):
            origin = source_ref[at_row, s]

            def fill(get, s=s):
                for t in range(slots):
                    there = slice(t * block, (t + 1) * block)
                    at = place_ref[at_row, s, t]

                    @pl.when(at >= 0)
                    def _():
                        for d in range(parts):
                            begin = s * block + d * rows
                            table[begin : begin + rows, there] = get(d, at).astype(held)

                    @pl.when(at < 0)
                    def _():
                        table[s * block : (s + 1) * block, there] = jnp.zeros((block, block), held)

            for chunk, (begin, end) in enumerate(starts):

                @pl.when((origin >= begin) & (origin < end))
                def _(chunk=chunk, begin=begin):
                    fill(lambda d, at: right_refs[chunk][d, origin - begin, at])

            for number in range(far):

                @pl.when(origin == starts[-1][1] + number)
                def _(number=number):
                    fill(lambda d, at: far_refs[number][at, d])

        near = jnp.concatenate(
            [
                jnp.concatenate([left_refs[m][n, t].astype(held) for m, n in pieces], axis=0)
                for t in range(slots)
            ],
            axis=1,
        ).astype(BF16)
        sums = lax.dot_general(
            near,
            table[...].astype(BF16),
            (((1,), (1,)), ((), ())),
            preferred_element_type=F32,
        )
        for d, (m, n) in enumerate(pieces):
            for s in range(slots):
                piece = sums[d * rows : (d + 1) * rows, s * block : (s + 1) * block]
                out_refs[m][n, s] = piece.astype(BF16)

    smem = pl.BlockSpec(memory_space=pltpu.SMEM)
    row_specs = [
        pl.BlockSpec(
            (left.shape[0], None, slots, None, rows, block), lambda c, i: (0, i, 0, c, 0, 0)
        )
        for left in lefts
    ]
    far_spec = pl.BlockSpec(
        arrived[0].shape[:2] + (None, rows, block), lambda c, i: (0, 0, c, 0, 0)
    )
    return pl.pallas_call(
        body,
        grid=(part, count),
        in_specs=[smem] * 2
        + row_specs
        + [
            pl.BlockSpec(right.shape[:3] + (None, rows, block), lambda c, i: (0, 0, 0, c, 0, 0))
            for right in rights
        ]
        + [far_spec] * far
        + [pl.BlockSpec(memory_space=pl.ANY)] * len(earlier),
        out_specs=row_specs,
        out_shape=[jax.ShapeDtypeStruct(left.shape, BF16) for left in lefts],
        scratch_shapes=[pltpu.VMEM((slots * block, slots * block), held)],
        compiler_params=params(),
        name=f"triangle_{first}",
    )(source, place, *lefts, *rights, *arrived, *earlier)


def attend(queries, cots, keys, values, bias_rows, places, masks, flags, chain_bias, *earlier):
    block_rows, rows, width = queries.shape
    heads = chain_bias.shape[0]
    _, slots, _, block = bias_rows[0].shape
    chunks = len(bias_rows)
    chunk_of = [
        (chunk, I - begin)
        for chunk, (begin, end) in enumerate(chunk_starts(bias_rows, 0))
        for I in range(begin, end)
    ]
    head_size = width // heads
    score_scale = head_size ** (-0.5)

    def body(place_ref, mask_ref, flag_ref, q_ref, c_ref, k_ref, v_ref, chain_ref, *refs):
        bias_refs, (mixed_ref, grad_ref) = refs[:chunks], refs[-2:]
        row_head = lax.broadcasted_iota(jnp.int32, (heads, width), 0)
        lane_head = lax.broadcasted_iota(jnp.int32, (heads, width), 1) // head_size
        own_head = (row_head == lane_head).astype(F32)
        chain = jnp.concatenate([chain_ref[...]] * rows, axis=0)
        for I, (chunk, inner) in enumerate(chunk_of):

            def spread(ref):
                wide = ref[I].astype(F32)
                return jnp.concatenate(
                    [
                        (jnp.broadcast_to(wide[i : i + 1], (heads, width)) * own_head).astype(BF16)
                        for i in range(rows)
                    ],
                    axis=0,
                )

            q_wide, c_wide = spread(q_ref), spread(c_ref)
            scores, grads = [], []
            for s in range(slots):
                near = place_ref[I, s]
                score = lax.dot_general(
                    q_wide, k_ref[near], (((1,), (1,)), ((), ())), preferred_element_type=F32
                )
                score = score * score_scale + bias_refs[chunk][inner, s].astype(F32) + chain * flag_ref[I, s]
                scores.append(jnp.where(mask_ref[I, s] > 0, score, -jnp.inf))
                grads.append(
                    lax.dot_general(
                        c_wide, v_ref[near], (((1,), (1,)), ((), ())), preferred_element_type=F32
                    )
                )
            scores = jnp.concatenate(scores, axis=1)
            grads = jnp.concatenate(grads, axis=1)
            exps = jnp.exp(scores - jnp.max(scores, axis=1, keepdims=True))
            probs = exps / jnp.sum(exps, axis=1, keepdims=True)
            low = probs.astype(BF16)
            mixed = jnp.zeros((rows * heads, width), F32)
            for s in range(slots):
                mixed = mixed + jnp.dot(
                    low[:, s * block : (s + 1) * block],
                    v_ref[place_ref[I, s]],
                    preferred_element_type=F32,
                )
            mixed = mixed.reshape(rows, heads, width) * own_head[None]
            mixed_ref[I] = jnp.sum(mixed, axis=1).astype(BF16)
            total = jnp.sum(probs * grads, axis=1, keepdims=True)
            score_grads = (probs * (grads - total)).astype(BF16)
            for s in range(slots):
                grad_ref[I, s] = score_grads[:, s * block : (s + 1) * block]

    smem = pl.BlockSpec(memory_space=pltpu.SMEM)
    vmem = pl.BlockSpec(memory_space=pltpu.VMEM)
    return pl.pallas_call(
        body,
        in_specs=[smem] * 3
        + [vmem] * (5 + chunks)
        + [pl.BlockSpec(memory_space=pl.ANY)] * len(earlier),
        out_specs=[vmem, vmem],
        out_shape=[
            jax.ShapeDtypeStruct((block_rows, rows, width), BF16),
            jax.ShapeDtypeStruct((block_rows, slots, rows * heads, block), BF16),
        ],
        compiler_params=params(),
        name="attend",
    )(places, masks, flags, queries, cots, keys, values, chain_bias, *bias_rows, *earlier)


def gradient_rows(pair_feats, grads, bias_rows, gate_half, back_weight, heads, first, earlier):
    count = bias_rows.shape[0]
    slots, rows, block, channels = pair_feats.shape[1:]

    def body(x_ref, g_ref, b_ref, gate_ref, back_ref, *refs):
        out_ref, grad_ref = refs[-2:]
        gate_weight, back = gate_ref[...], back_ref[...]
        for i in range(rows):
            xhat, scale = norm_parts(x_ref[i].astype(F32), 1)
            gate = jnp.dot(xhat.astype(BF16), gate_weight, preferred_element_type=F32)
            out_ref[i] = (0.5 * jnp.tanh(gate) + 0.5).astype(BF16)
            g = g_ref[i * heads : (i + 1) * heads]
            b = b_ref[i * heads : (i + 1) * heads]
            cross = jnp.sum(g.astype(F32) * b.astype(F32), axis=0, keepdims=True) / channels
            cross = jnp.broadcast_to(cross, (heads, block)).astype(BF16)
            both = lax.dot_general(
                jnp.concatenate([g, cross], axis=0),
                back,
                (((0,), (0,)), ((), ())),
                preferred_element_type=F32,
            )
            centred, projection = both[:, :channels], both[:, channels:]
            grad_ref[i] = (scale * (centred - xhat * projection)).astype(BF16)

    big = pl.BlockSpec((None, None, rows, block, channels), lambda i, s: (first + i, s, 0, 0, 0))
    whole = jax.ShapeDtypeStruct(pair_feats.shape, BF16)
    anywhere = pl.BlockSpec(memory_space=pl.ANY)
    return pl.pallas_call(
        body,
        grid=(count, slots),
        in_specs=[
            big,
            pl.BlockSpec((None, None, rows * heads, block), lambda i, s: (first + i, s, 0, 0)),
            pl.BlockSpec((None, None, rows * heads, block), lambda i, s: (i, s, 0, 0)),
            pl.BlockSpec(gate_half.shape, lambda i, s: (0, 0)),
            pl.BlockSpec(back_weight.shape, lambda i, s: (0, 0)),
        ]
        + [anywhere] * len(earlier),
        out_specs=[big, big],
        out_shape=[whole, whole],
        input_output_aliases={5 + n: n for n in range(len(earlier))},
        compiler_params=params(),
        name=f"gradient_{first}",
    )(pair_feats, grads, bias_rows, gate_half, back_weight, *earlier)


def finish_rows(pair_feats, gates, near_tris, tri, tri_out_weight, place, first):
    slots, rows, block, channels = pair_feats.shape[1:]
    parts, count, _, part, _, _ = tri.shape
    span, near_part = len(near_tris), near_tris[0].shape[3]
    near = span * near_part
    hidden = near + parts * part

    def body(place_ref, x_ref, gate_ref, *refs):
        near_refs, (tri_ref, w_ref, out_ref, buf) = refs[:span], refs[span:]
        for d in range(span):
            here = pl.ds((place_ref[0] ^ d) * near_part, near_part)
            buf[here] = near_refs[d][...].astype(F32)
        buf[near:] = tri_ref[...].astype(F32).reshape(parts * part, rows, block)
        buf[...] = norm_parts(buf[...], 0)[0]
        weight = w_ref[...]
        for i in range(rows):
            update = lax.dot_general(
                buf[:, i, :].astype(BF16),
                weight,
                (((0,), (0,)), ((), ())),
                preferred_element_type=F32,
            )
            out_ref[i] = (x_ref[i].astype(F32) + gate_ref[i].astype(F32) * update).astype(BF16)

    big = pl.BlockSpec((None, None, rows, block, channels), lambda i, s: (first + i, s, 0, 0, 0))
    return pl.pallas_call(
        body,
        grid=(count, slots),
        in_specs=[pl.BlockSpec(memory_space=pltpu.SMEM), big, big]
        + [
            pl.BlockSpec(
                (None, None, None, near_part, rows, block), lambda i, s: (0, i, s, 0, 0, 0)
            )
        ]
        * span
        + [
            pl.BlockSpec(
                (parts, None, None, part, rows, block), lambda i, s: (0, i, s, 0, 0, 0)
            ),
            pl.BlockSpec(tri_out_weight.shape, lambda i, s: (0, 0)),
        ],
        out_specs=big,
        out_shape=jax.ShapeDtypeStruct(pair_feats.shape, BF16),
        input_output_aliases={2: 0},
        scratch_shapes=[pltpu.VMEM((hidden, rows, block), F32)],
        compiler_params=params(),
        name=f"finish_{first}",
    )(place, pair_feats, gates, *near_tris, tri, tri_out_weight)


def after(values, *earlier):
    return lax.optimization_barrier((values,) + earlier)[0]


def doubling_steps(axis):
    size = lax.axis_size(axis)
    return [size >> n for n in range(1, size.bit_length())]


def doubled(stacked, axis, steps):
    size = lax.axis_size(axis)
    for step in steps:
        pairs = [(n, n ^ step) for n in range(size)]
        stacked = jnp.concatenate([stacked, lax.ppermute(stacked, axis, pairs)], axis=0)
    return stacked


def doubled_order(axis):
    away = jnp.arange(lax.axis_size(axis), dtype=jnp.int32) ^ lax.axis_index(axis)
    order = jnp.zeros_like(away)
    for number, step in enumerate(doubling_steps(axis)):
        order = order + jnp.where(away & step, 1 << number, 0)
    return order


def make_plan(block_cols, group_index, group_count, block_rows):
    total_rows, slots = block_cols.shape
    offsets = group_count - 1
    cap_slots = slots - block_rows + CAPX
    first_row = group_index * block_rows
    targets = jnp.arange(total_rows, dtype=jnp.int32)
    owner = targets // block_rows
    groups = jnp.arange(group_count, dtype=jnp.int32)
    hits = (block_cols[:, :, None] == targets).astype(jnp.int32)
    union = jnp.max(hits.reshape(group_count, block_rows * slots, total_rows), axis=1)
    named = union * (owner[None, :] != groups[:, None]).astype(jnp.int32)
    by_owner = named.reshape(group_count, group_count, block_rows)
    row_rank = (jnp.cumsum(by_owner, axis=2) - by_owner).reshape(group_count, total_rows)
    useful = jnp.max(union[:, None, None, :] * hits[None], axis=3)
    slot_rank = jnp.cumsum(useful, axis=2) - useful
    to_group = (group_index + 1 + jnp.arange(offsets, dtype=jnp.int32)) % group_count
    locals_ = jnp.arange(block_rows, dtype=jnp.int32)
    named_here = lax.dynamic_slice_in_dim(named, first_row, block_rows, 1)[to_group]
    rank_here = lax.dynamic_slice_in_dim(row_rank, first_row, block_rows, 1)[to_group]
    caps = jnp.arange(CAPX, dtype=jnp.int32)
    chosen = named_here[:, None, :] * (rank_here[:, None, :] == caps[None, :, None])
    send_row = jnp.sum(chosen * locals_, axis=2).astype(jnp.int32)
    useful_here = lax.dynamic_slice_in_dim(useful, first_row, block_rows, 1)[to_group]
    srank_here = lax.dynamic_slice_in_dim(slot_rank, first_row, block_rows, 1)[to_group]
    cap_ids = jnp.arange(cap_slots, dtype=jnp.int32)
    slot_ids = jnp.arange(slots, dtype=jnp.int32)
    picks = useful_here[:, :, None, :] * (
        srank_here[:, :, None, :] == cap_ids[None, None, :, None]
    )
    slot_of = jnp.sum(picks * slot_ids, axis=3)
    send_slot = jnp.sum(chosen[:, :, :, None] * slot_of[:, None, :, :], axis=2).astype(jnp.int32)
    my_rank = lax.dynamic_index_in_dim(row_rank, group_index, 0, keepdims=False)
    my_slot_rank = lax.dynamic_index_in_dim(slot_rank, group_index, 0, keepdims=False)
    distance = (group_index - owner) % group_count
    is_local = distance == 0
    row_source = jnp.where(is_local, targets - first_row, block_rows + distance - 1)
    node_place = jnp.where(
        is_local, targets - first_row, block_rows + (distance - 1) * CAPX + my_rank
    )
    own_cols = lax.dynamic_slice_in_dim(block_cols, first_row, block_rows, 0)
    near_cols = block_cols[own_cols]
    match = near_cols[:, :, None, :] == own_cols[:, None, :, None]
    found = jnp.max(match.astype(jnp.int32), axis=3)
    slot_place = jnp.where(
        is_local[:, None], slot_ids[None, :], my_rank[:, None] * cap_slots + my_slot_rank
    )
    place = jnp.sum(match.astype(jnp.int32) * slot_place[own_cols][:, :, None, :], axis=3)
    tri_place = jnp.where(found > 0, place, -1).astype(jnp.int32)
    tri_source = row_source[own_cols].astype(jnp.int32)
    return (send_row, send_slot, own_cols, tri_source, tri_place, node_place.astype(jnp.int32))


def per_device(
    pair_feats,
    block_cols,
    attn_mask,
    chain_of_row,
    same_chain,
    node_feats,
    node_cotangent,
    tri_weight,
    gate_weight,
    tri_out_weight,
    bias_weight,
    query_weight,
    key_weight,
    value_weight,
    out_weight,
):
    parts = lax.axis_size("row")
    group_count = lax.axis_size("grp")
    group_index = lax.axis_index("grp")
    row_index = lax.axis_index("row")
    block_rows, slots, rows, block, channels = pair_feats.shape
    hidden = tri_weight.shape[1] // 4
    heads = bias_weight.shape[1]
    width = node_feats.shape[1]
    offsets = group_count - 1
    first_row = group_index * block_rows
    send_row, send_slot, own_cols, tri_source, tri_place, node_place = make_plan(
        block_cols, group_index, group_count, block_rows
    )
    rings = [
        [(g, (g + d) % group_count) for g in range(group_count)] for d in range(1, group_count)
    ]

    weights_t = jnp.concatenate([tri_weight.T * 0.5, bias_weight.T], axis=0).astype(BF16)
    own_weights = jnp.stack([query_weight.T, key_weight.T, value_weight.T, out_weight])
    share = own_weights.shape[0] * own_weights.shape[1] // group_count
    own_share = lax.dynamic_slice_in_dim(
        own_weights.reshape(-1, width), group_index * share, share, 0
    )
    row_steps = doubling_steps("row")
    near_share = doubled(own_share[None], "row", row_steps[:1])

    def swap(values, *earlier):
        return lax.all_to_all(
            after(values, *earlier), "row", split_axis=0, concat_axis=0, tiled=True
        )

    groups = [(0, LEAD), (LEAD, block_rows - LEAD)]
    left_near_0, left_0, right_near_0, right_0, bias_0 = project_rows(
        pair_feats, weights_t, parts, *groups[0], heads
    )
    right_near_0 = swap(right_near_0, near_share)
    left_near_1, left_1, right_near_1, right_1, bias_1 = project_rows(
        pair_feats, weights_t, parts, *groups[1], heads
    )
    biases = (bias_0, bias_1)
    half_share = doubled(near_share, "row", row_steps[1:-1])
    right_near_1 = swap(right_near_1, right_near_0, half_share)
    rights_near = [right_near_0, right_near_1]
    row_share = doubled(half_share, "row", row_steps[-1:])
    all_stack = jnp.swapaxes(doubled(row_share[None], "grp", doubling_steps("grp")), 0, 1)
    row_order, grp_order = doubled_order("row"), doubled_order("grp")
    plan_parts = (send_row, send_slot, node_place, tri_source, tri_place)
    span = parts // 2
    half_place = row_index % span

    def pairwise(pieces):
        return [pieces[0]] + [
            lax.ppermute(pieces[d], "row", [(r, r ^ d) for r in range(parts)])
            for d in range(1, span)
        ]

    def pieces_of(stacked):
        return [
            lax.dynamic_slice_in_dim(stacked, half_place ^ d, 1, 0) for d in range(span)
        ]

    left_near_1 = pairwise(pieces_of(left_near_1))
    left_near_0 = pairwise(pieces_of(left_near_0))
    right_all = swap(
        jnp.concatenate([right_0, right_1], axis=1), right_near_1, all_stack, *plan_parts, *left_near_0, *left_near_1
    )
    rights = [right_all]
    outgoing_near = pick_blocks(rights_near, send_row, send_slot, offsets)
    arrived_near = [lax.ppermute(v, "grp", ring) for v, ring in zip(outgoing_near, rings)]
    all_stack = after(all_stack, *outgoing_near)

    all_weights = all_stack[row_order[:, None], grp_order[None, :]].reshape(
        (parts,) + own_weights.shape
    )

    def full(number):
        return all_weights[:, number].reshape(width, width)

    node_norm = norm_parts(node_feats.astype(F32), 1)[0].astype(BF16)
    norm_blocks = node_norm.reshape(block_rows, block, width)
    far_nodes = [
        lax.ppermute(norm_blocks[send_row[d]], "grp", rings[d]) for d in range(offsets)
    ]
    near_nodes = jnp.concatenate([norm_blocks] + far_nodes, axis=0).reshape(-1, width)

    def times_t(values, weight):
        return lax.dot_general(
            values, weight, (((1,), (1,)), ((), ())), preferred_element_type=F32
        ).astype(BF16)

    keys = times_t(near_nodes, full(1)).reshape(-1, block, width)
    values = times_t(near_nodes, full(2)).reshape(-1, block, width)

    def own_rows(array):
        return lax.dynamic_slice_in_dim(
            array.reshape(block_rows, block, width), row_index * rows, rows, 1
        ).reshape(block_rows * rows, width)

    queries = times_t(own_rows(node_norm), full(0)).reshape(block_rows, rows, width)
    cots = times_t(own_rows(node_cotangent), full(3)).reshape(block_rows, rows, width)
    own_chain = lax.dynamic_slice_in_dim(chain_of_row, first_row, block_rows, 0)
    masks = lax.dynamic_slice_in_dim(attn_mask, first_row, block_rows, 0)
    flags = (chain_of_row[own_cols] == own_chain[:, None]).astype(F32)
    chain_bias = jnp.broadcast_to(same_chain[:, None], (heads, block))
    mixed, grads = attend(
        queries,
        cots,
        keys,
        values,
        biases,
        node_place[own_cols],
        masks,
        flags,
        chain_bias,
        arrived_near[0],
    )

    bias_float = bias_weight.astype(F32)
    centred = (bias_float - jnp.mean(bias_float, axis=0, keepdims=True)).T
    zeros = jnp.zeros((heads, channels), F32)
    back_weight = jnp.concatenate(
        [
            jnp.concatenate([centred, zeros], axis=1),
            jnp.concatenate([zeros, zeros + 1.0 / heads], axis=1),
        ],
        axis=0,
    ).astype(BF16)
    gate_half = (gate_weight * 0.5).astype(BF16)
    whole = ()
    for (first, _), bias in zip(groups, biases):
        whole = gradient_rows(
            pair_feats, grads, bias, gate_half, back_weight, heads, first, whole
        )
    pair_out, pair_grad = whole

    left_rest = swap(left_1, right_all, mixed)
    outgoing = pick_blocks(rights, send_row, send_slot, offsets)
    arrived = [lax.ppermute(v, "grp", ring) for v, ring in zip(outgoing, rings)]
    near_mixed = mixed[None]
    for step in [1 << n for n in range(block_rows.bit_length() - 1)]:
        other = lax.ppermute(near_mixed, "row", [(r, r ^ step) for r in range(parts)])
        swapped = (row_index & step) > 0
        near_mixed = jnp.concatenate(
            [jnp.where(swapped, other, near_mixed), jnp.where(swapped, near_mixed, other)], axis=0
        )
    left_lead = swap(left_0, left_rest, near_mixed, pair_grad, *outgoing)
    sharers = parts // block_rows
    sent_mixed = lax.dynamic_index_in_dim(near_mixed, row_index % block_rows, 1, keepdims=False)
    senders = [((r % sharers) * block_rows + r // sharers, r) for r in range(parts)]
    node_rows = block_rows * block // parts
    mixed_own = lax.ppermute(sent_mixed, "row", senders).reshape(node_rows, width)
    near_args = (rights_near, arrived_near, tri_source, tri_place)
    args = (rights, arrived, tri_source, tri_place)
    near_sums_1 = triangle_rows(left_near_1, *near_args, LEAD, pair_grad, *outgoing)
    near_rest = pairwise(near_sums_1)
    sums = triangle_rows([left_rest], *args, LEAD, near_sums_1[0])[0]
    tri_rest = swap(sums, left_lead)
    near_sums_0 = triangle_rows(left_near_0, *near_args, 0, sums)
    near_lead = pairwise(near_sums_0)
    sums = triangle_rows([left_lead], *args, 0, near_sums_0[0], mixed_own)[0]
    tri_lead = swap(sums, tri_rest, *near_rest)
    own_nodes = lax.dynamic_slice_in_dim(node_feats, row_index * node_rows, node_rows, 0)
    node_out = (
        own_nodes.astype(F32) + jnp.dot(mixed_own, full(3), preferred_element_type=F32)
    ).astype(BF16)
    tri_lead = after(tri_lead, node_out)
    place = half_place.reshape(1).astype(jnp.int32)
    pair_out = finish_rows(
        pair_feats, pair_out, near_rest, tri_rest, tri_out_weight, place, LEAD
    )
    pair_out = finish_rows(pair_feats, pair_out, near_lead, tri_lead, tri_out_weight, place, 0)
    return (pair_out, node_out, pair_grad)


def solution(mesh):
    pair_spec = P("grp", None, "row", None, None)
    in_specs = (
        (pair_spec,)
        + (P(),) * 4
        + (P("grp", None),) * 2
        + (P(),) * 4
        + (P(None, "row"),) * 3
        + (P("row", None),)
    )
    out_specs = (pair_spec, P(("grp", "row"), None), pair_spec)
    return jax.shard_map(
        per_device, mesh=mesh, in_specs=in_specs, out_specs=out_specs, check_vma=False
    )
```
